256 devices in a mesh: dp: 2 (over core), seq: 8 (over z), expert: 16 (over y, x).
Axes of the slice: x: 4, y: 4, z: 8, core: 2. Of those that a mesh axis runs over, the one named last changes fastest.
Arguments:
- tokens: bfloat16 [16, 2048, 2560], P(('dp', 'seq'), 'expert'), may hold values from -6 to 6
- text_states: bfloat16 [16, 128, 4096], P('dp', None, 'seq'), may hold values from -6 to 6
- text_lengths: int32 [16], P('dp'), may hold values from 64 to 128
- mod_weight: bfloat16 [4096, 5120], P('seq', 'expert'), may hold values from -1 to 1
- router_weight: bfloat16 [2560, 4], replicated, may hold values from -0.125 to 0.125
- gate_weight: bfloat16 [2560, 13824], P('dp', 'expert'), may hold values from -0.125 to 0.125
- up_weight: bfloat16 [2560, 13824], P('dp', 'expert'), may hold values from -0.125 to 0.125
- down_weight: bfloat16 [13824, 2560], P('expert', 'dp'), may hold values from -0.109375 to 0.109375
- expert_ids: int32 [16, 2048, 2], P(('dp', 'seq'), 'expert'), may hold values from 0 to 3, all different within a row; in each aligned block of 128 rows (0 to 127, 128 to 255, ..., all dimensions but the last counted through in order) at most 68 rows name the same one
- dropped: int32 [16, 2048, 2], P(('dp', 'seq'), 'expert'), may hold values 0 or 1
Outputs:
- mixed: bfloat16 [16, 2048, 2560], P(('dp', 'seq'), 'expert')
The draws below stay inside these ranges and needn't reach their ends.
Inputs may be any that keep to these rules, and one draw needn't show every extreme that they name: `expert_ids`: each row names 2 different experts. In every aligned block of 128 patches (one image's patches on one device) no expert is named by more than 68 rows, and some block reaches 68.
All inputs are finite; a program needn't handle non-finite values. No bound on the sum of `dropped` on one device may be relied on, other than what follows from the above.
Results may differ from the reference program's by a relative error of at most 0.014.
Values may be sent and summed in bfloat16 or wider, within the bound.
No kernel may reach another device: no remote copies, remote signals or barrier semaphores. Data moves between devices by JAX's collectives and lax.ppermute only.
A program may use at most 128 MiB of HBM per device.

```python
import math
import jax
import jax.numpy as jnp
import numpy as np
from jax import lax

D = 2560
DT = 4096
FF = 3456
EXPERTS = 4
TOP = 2
LTXT = 128
PATCH_DEV = 128
MOST = 68
IMAGES = 16
PATCHES = 2048
SPLIT = 4
FQ = 864


def set_ends(entries, key, least, top_value):
    shape = entries.shape
    spot = [jax.random.randint(jax.random.fold_in(key, axis), (), 0, shape[axis]) for axis in range(len(shape))]
    entries = entries.at[tuple(spot)].set(least)
    longest = shape.index(max(shape))
    spot[longest] = (spot[longest] + 1) % shape[longest]
    return entries.at[tuple(spot)].set(top_value)


def block_levels(rng, shape, cuts, low, largest):
    factor_of = 1.0
    for position, blocks in cuts:
        draws = jax.random.uniform(jax.random.fold_in(jax.random.fold_in(rng, 6), position), (blocks,), jnp.float32, low / len(cuts), largest / len(cuts))
        factor_of = factor_of * jnp.repeat(jnp.exp(draws), shape[position] // blocks).reshape((-1,) + (1,) * (len(shape) - 1 - position))
    return factor_of


def deal_out(own_key, own, number, rows, count, top, reach, slope):
    order = jax.random.permutation(own_key, count)
    packed, common = load_shares(count, rows * top, reach, slope, True), load_shares(count, rows * top, reach, slope, False)
    places = jnp.arange(count)

    def named(tallies, rotation):
        used = int((tallies > 0).sum())
        fixed = max(1, used // 4)
        shifted = fixed + (places - fixed + rotation * (used - fixed)) % max(1, count - fixed)
        return jnp.zeros((count,), jnp.int32).at[order[jnp.where(places < fixed, places, shifted)]].set(jnp.asarray(tallies, jnp.int32))

    tallies = jnp.where(number % 4 == 0, named(packed, number // 4), named(common, number - number // 4 - 1))
    mixed = jax.random.permutation(jax.random.fold_in(own, 3), count)
    giver, receiver = mixed[0:count // 2 * 2:2], mixed[1:count // 2 * 2:2]
    slack = jnp.minimum(tallies[giver] - 1, reach - tallies[receiver]) // 2
    slack = jnp.where((giver == order[0]) | (receiver == order[0]) | (tallies[receiver] == 0), 0, jnp.maximum(slack, 0))
    shifted = jax.random.randint(jax.random.fold_in(own, 4), (count // 2,), 0, 1 << 20) % (slack + 1)
    tallies = tallies.at[giver].add(-shifted).at[receiver].add(shifted)
    items = jnp.searchsorted(jnp.cumsum(tallies), jnp.arange(rows * top), side="right").astype(jnp.int32)
    listing = items.reshape(top, rows).T
    listing = listing[jax.random.permutation(jax.random.fold_in(own, 1), rows)]
    rotation = jax.random.randint(jax.random.fold_in(own, 2), (rows, 1), 0, top)
    return jnp.take_along_axis(listing, (jnp.arange(top)[None, :] + rotation) % top, axis=1)


def load_shares(number_of, total, bound, skew, full):
    loads = [(1 << 20) // math.isqrt(grade ** skew) + 1 for grade in range(1, number_of + 1)]
    largest = bound if full else min(bound, max(-(-total // number_of), total * loads[0] // sum(loads)))
    least = 1 if total - largest >= number_of - 1 else 0
    given, spare = [largest] + [least] * (number_of - 1), total - largest - least * (number_of - 1)
    while spare > 0:
        free = [i for i in range(1, number_of) if given[i] < largest] or [i for i in range(1, number_of) if given[i] < bound]
        pool, budget = sum([loads[i] for i in free]), spare
        for i in free:
            addition = min(bound - given[i], max(1, budget * loads[i] // pool), spare)
            given[i] = given[i] + addition
            spare = spare - addition
    return np.array(given)


def noise(own_key, shape, scale, bound, cuts=(), kind=jnp.bfloat16):
    loudness = block_levels(own_key, shape, cuts, -0.22, 0.18) if cuts else 1.0
    array = jax.random.normal(own_key, shape, jnp.float32) * scale * loudness
    return jnp.minimum(jnp.maximum(array, -bound), bound).astype(kind)


def setup_inputs(seed: int = 0) -> dict:
    splits = jax.random.split(jax.random.key(seed), 11)
    tokens = noise(splits[0], (IMAGES, PATCHES, D), 1.0, 6.0, ((0, 16), (1, 16)))
    text_states = noise(splits[1], (IMAGES, LTXT, DT), 1.0, 6.0, ((0, 2), (2, 8)))
    text_lengths = set_ends(jax.random.randint(splits[2], (IMAGES,), LTXT // 2, LTXT + 1), jax.random.fold_in(splits[2], 1), LTXT // 2, LTXT).astype(jnp.int32)
    mod_weight = noise(splits[3], (DT, 2 * D), (DT // LTXT) ** -0.5, 1.0, ((0, 8), (1, 16)))
    router_weight = noise(splits[4], (D, EXPERTS), D ** -0.5, 0.125)
    gate_weight = noise(splits[5], (D, EXPERTS * FF), D ** -0.5, 0.125, ((0, 2), (1, 16)))
    up_weight = noise(splits[6], (D, EXPERTS * FF), D ** -0.5, 0.125, ((0, 2), (1, 16)))
    down_weight = noise(splits[7], (EXPERTS * FF, D), FF ** -0.5, 0.109375, ((0, 16), (1, 2)))
    expert_ids_keys = jax.random.split(jax.random.fold_in(splits[8], 1), IMAGES * PATCHES // PATCH_DEV)
    expert_ids_turns = jax.random.permutation(jax.random.fold_in(splits[8], 3), IMAGES * PATCHES // PATCH_DEV)
    expert_ids = jax.vmap(lambda own, number: deal_out(jax.random.fold_in(splits[8], 2), own, number, PATCH_DEV, EXPERTS, TOP, MOST, 1))(expert_ids_keys, expert_ids_turns).reshape((IMAGES, PATCHES, TOP))
    dropped = set_ends((jax.random.randint(splits[9], (IMAGES, PATCHES, TOP), 0, 8) < 1).astype(jnp.int32), jax.random.fold_in(splits[9], 1), 0, 1)
    return {"tokens": tokens, "text_states": text_states, "text_lengths": text_lengths, "mod_weight": mod_weight, "router_weight": router_weight, "gate_weight": gate_weight, "up_weight": up_weight, "down_weight": down_weight, "expert_ids": expert_ids, "dropped": dropped}


def slot_rank(choices):
    total = choices.shape[0]
    hits = (choices[:, :, None] == jnp.arange(EXPERTS, dtype=jnp.int32)[None, None, :]).astype(jnp.int32)
    blocks = hits.reshape(total // PATCH_DEV, PATCH_DEV * TOP, EXPERTS)
    before = jnp.cumsum(blocks, axis=1) - blocks
    return lax.optimization_barrier(jnp.sum(before * blocks, axis=2)).reshape(total, TOP).astype(jnp.int32)

def reference(tokens, text_states, text_lengths, mod_weight, router_weight, gate_weight, up_weight, down_weight, expert_ids, dropped):
    positions = jnp.arange(LTXT, dtype=jnp.int32)
    valid = (positions[None, :] < text_lengths[:, None]).astype(jnp.float32)
    pooled = jnp.einsum('it,itc->ic', valid, text_states.astype(jnp.float32))
    pooled = (pooled / text_lengths.astype(jnp.float32)[:, None]).astype(jnp.bfloat16)
    modulation = jnp.dot(pooled, mod_weight, preferred_element_type=jnp.float32)
    scale = modulation[:, :D]
    shift = modulation[:, D:]
    values = tokens.astype(jnp.float32)
    centre = lax.optimization_barrier(jnp.mean(values, axis=2, keepdims=True))
    spread = lax.optimization_barrier(jnp.mean((values - centre) ** 2, axis=2, keepdims=True))
    normed = (values - centre) * lax.rsqrt(spread + 1e-06)
    hidden_in = (normed * (1.0 + scale[:, None, :]) + shift[:, None, :]).astype(jnp.bfloat16)
    total = IMAGES * PATCHES
    flat = hidden_in.reshape(total, D)
    gates = jax.nn.sigmoid(jnp.dot(flat, router_weight, preferred_element_type=jnp.float32))
    choices = expert_ids.reshape(total, TOP).astype(jnp.int32)
    weight = jnp.take_along_axis(gates, choices, axis=1) * (1 - dropped.reshape(total, TOP)).astype(jnp.float32)
    block = (jnp.arange(total, dtype=jnp.int32) // PATCH_DEV)[:, None]
    slot = block * MOST + slot_rank(choices)
    slots_all = total // PATCH_DEV * MOST
    row_index = jnp.broadcast_to(jnp.arange(total, dtype=jnp.int32)[:, None], (total, TOP))
    source = jnp.full((EXPERTS, slots_all), total, jnp.int32).at[choices, slot].set(row_index)
    slot_weight = jnp.zeros((EXPERTS, slots_all), jnp.float32).at[choices, slot].set(weight)
    padded = jnp.concatenate([flat, jnp.zeros((1, D), jnp.bfloat16)], axis=0)
    gate_stack = gate_weight.reshape(D, EXPERTS, FF).transpose(1, 0, 2)
    up_stack = up_weight.reshape(D, EXPERTS, FF).transpose(1, 0, 2)
    down_stack = down_weight.reshape(EXPERTS, FF, D)

    def one_expert(carry, pieces):
        src, wts, w_gate, w_up, w_down = pieces
        rows = jnp.take(padded, src, axis=0)
        gate = jnp.dot(rows, w_gate, preferred_element_type=jnp.float32)
        upper = jnp.dot(rows, w_up, preferred_element_type=jnp.float32)
        hidden = (jax.nn.silu(gate) * upper).astype(jnp.bfloat16)
        summed = jnp.zeros((src.shape[0], D), jnp.float32)
        for group in range(SPLIT):
            part = jnp.dot(hidden[:, group * FQ:(group + 1) * FQ], w_down[group * FQ:(group + 1) * FQ], preferred_element_type=jnp.float32)
            rounded = lax.optimization_barrier((part * wts[:, None]).astype(jnp.bfloat16))
            summed = summed + rounded.astype(jnp.float32)
        return (carry.at[src].add(summed), None)
    start = jnp.zeros((total + 1, D), jnp.float32)
    gathered, unused = lax.scan(one_expert, start, (source, slot_weight, gate_stack, up_stack, down_stack))
    result = values + gathered[:total].reshape(IMAGES, PATCHES, D)
    return result.astype(jnp.bfloat16)
```

```python
import functools

import jax
import jax.numpy as jnp
from jax import lax
from jax.experimental import pallas as pl
from jax.experimental.pallas import tpu as pltpu
from jax.sharding import PartitionSpec as P

SIDE = 4
SLOTS = 72
CHUNKS = ((0,), (1, -1, 2))
OFFSETS = (0, 1, -1, 2)
VMEM_LIMIT = 56 * 1024 * 1024


def along_x(step):
    return [
        (y * SIDE + x, y * SIDE + (x + step) % SIDE) for y in range(SIDE) for x in range(SIDE)
    ]


def along_y(step):
    return [
        (y * SIDE + x, ((y + step) % SIDE) * SIDE + x) for y in range(SIDE) for x in range(SIDE)
    ]


def shift(value, perm):
    return lax.ppermute(value, "expert", perm)


def bin_kernel(y_ref, ids_ref, tokens_ref, normed_ref, *bin_refs):
    rows, width = tokens_ref.shape
    for start in range(0, rows, 16):
        block = tokens_ref[start : start + 16, :].astype(jnp.float32)
        centre = jnp.sum(block, axis=1, keepdims=True) * (1.0 / width)
        block = block - centre
        spread = jnp.sum(block * block, axis=1, keepdims=True) * (1.0 / width)
        normed_ref[start : start + 16, :] = (block * lax.rsqrt(spread + 1e-06)).astype(
            jnp.bfloat16
        )
    before = (
        lax.broadcasted_iota(jnp.int32, (rows, rows), 0)
        < lax.broadcasted_iota(jnp.int32, (rows, rows), 1)
    ).astype(jnp.bfloat16)
    slot = lax.broadcasted_iota(jnp.int32, (SLOTS, rows), 0)
    normed = normed_ref[...]
    for offset, bin_ref in zip(OFFSETS, bin_refs):
        expert = lax.rem(y_ref[0] + offset + SIDE, SIDE)
        named = jnp.max((ids_ref[...] == expert).astype(jnp.float32), axis=0, keepdims=True)
        rank = jnp.dot(
            jnp.broadcast_to(named, (16, rows)).astype(jnp.bfloat16),
            before,
            preferred_element_type=jnp.float32,
        )[0:1, :].astype(jnp.int32)
        pick = jnp.where((slot == rank) & (named > 0.0), 1.0, 0.0).astype(jnp.bfloat16)
        bin_ref[...] = jnp.dot(pick, normed, preferred_element_type=jnp.float32).astype(
            jnp.bfloat16
        )


def make_bins(y_index, ids_rows, tokens):
    rows, width = tokens.shape
    vmem = pl.BlockSpec(memory_space=pltpu.VMEM)
    return pl.pallas_call(
        bin_kernel,
        out_shape=[jax.ShapeDtypeStruct((rows, width), jnp.bfloat16)]
        + [jax.ShapeDtypeStruct((SLOTS, width), jnp.bfloat16)] * len(OFFSETS),
        in_specs=[pl.BlockSpec(memory_space=pltpu.SMEM), vmem, vmem],
        out_specs=[vmem] * (1 + len(OFFSETS)),
        compiler_params=pltpu.CompilerParams(vmem_limit_bytes=VMEM_LIMIT),
        cost_estimate=pl.CostEstimate(
            flops=2 * 4 * SLOTS * rows * width, bytes_accessed=8 * rows * width, transcendentals=0
        ),
        name="normalise_and_bin",
    )(y_index, ids_rows, tokens)


def expert_kernel(
    dp_ref,
    mod_ref,
    own_ref,
    left_ref,
    right_ref,
    far_a_ref,
    far_b_ref,
    gate_own,
    gate_far,
    up_own,
    up_far,
    down_own,
    down_far,
    out_own,
    out_left,
    out_right,
    out_far_a,
    out_far_b,
    w_gate,
    w_up,
    w_down,
    acc_gate,
    acc_up,
    sems,
):
    width = own_ref.shape[2]
    half = width // 2
    tile = half // 2
    first = pl.program_id(0) == 0
    dp = dp_ref[0]

    def pieces():
        for part in range(4):
            bank, start = part // 2, (part % 2) * tile
            yield bank, gate_own, gate_far, w_gate, 0, pl.ds(start, tile), part
            yield bank, up_own, up_far, w_up, 0, pl.ds(start, tile), part
        for part in range(4):
            bank, start = part // 2, (part % 2) * tile
            yield bank, down_own, down_far, w_down, 1, pl.ds(start, tile), part

    def copies(source):
        for number, (bank, own, far, scratch, axis, span, part) in enumerate(pieces()):
            ref = (own if source == "own" else far) if source != "bank" else own
            index = (span, slice(None)) if axis == 0 else (slice(None), span)
            yield (
                number,
                bank,
                pltpu.make_async_copy(
                    ref.at[index], scratch.at[(bank,) + index], sems.at[number]
                ),
            )

    @pl.when(first)
    def _():
        for (number, bank, mine), (_, _, other) in zip(copies("own"), copies("far")):
            is_mine = dp == bank

            @pl.when(is_mine)
            def _(mine=mine):
                mine.start()

            @pl.when(jnp.logical_not(is_mine))
            def _(other=other):
                other.start()

    waits = [copy for _, _, copy in copies("own")]

    for part in range(4):

        @pl.when(first)
        def _(part=part):
            waits[2 * part].wait()
            waits[2 * part + 1].wait()

        bank, start = part // 2, (part % 2) * tile
        span = slice(part * tile, (part + 1) * tile)
        far_ref = far_a_ref if bank == 0 else far_b_ref
        values = jnp.concatenate(
            [
                own_ref[0, :, span].astype(jnp.float32),
                left_ref[0, :, span].astype(jnp.float32),
                right_ref[0, :, span].astype(jnp.float32),
                far_ref[0, :, start : start + tile].astype(jnp.float32),
            ],
            axis=0,
        )
        hidden_in = (values * (1.0 + mod_ref[0:1, span]) + mod_ref[1:2, span]).astype(jnp.bfloat16)
        gate = jnp.dot(
            hidden_in, w_gate[bank, start : start + tile, :], preferred_element_type=jnp.float32
        )
        upper = jnp.dot(
            hidden_in, w_up[bank, start : start + tile, :], preferred_element_type=jnp.float32
        )
        if part == 0:
            acc_gate[...] = gate
            acc_up[...] = upper
        else:
            acc_gate[...] += gate
            acc_up[...] += upper
    hidden = (jax.nn.silu(acc_gate[...]) * acc_up[...]).astype(jnp.bfloat16)
    for part in range(4):

        @pl.when(first)
        def _(part=part):
            waits[8 + part].wait()

        bank, start = part // 2, (part % 2) * tile
        span = slice(part * tile, (part + 1) * tile)
        out = jnp.dot(
            hidden, w_down[bank, :, start : start + tile], preferred_element_type=jnp.float32
        )
        out_own[0, :, span] = out[0:SLOTS].astype(jnp.bfloat16)
        out_left[0, :, span] = out[SLOTS : 2 * SLOTS].astype(jnp.bfloat16)
        out_right[0, :, span] = out[2 * SLOTS : 3 * SLOTS].astype(jnp.bfloat16)
        out_far = out_far_a if bank == 0 else out_far_b
        out_far[0, :, start : start + tile] = out[3 * SLOTS : 4 * SLOTS].astype(jnp.bfloat16)


def run_expert(dp_index, modulation, own, left, right, far_a, far_b, weights):
    count, slots, width = own.shape
    half = width // 2
    units = weights[0].shape[1]
    any_space = pl.BlockSpec(memory_space=pl.ANY)
    whole = pl.BlockSpec((1, slots, width), lambda i: (i, 0, 0))
    split = pl.BlockSpec((1, slots, half), lambda i: (i, 0, 0))
    wide = jax.ShapeDtypeStruct((count, slots, width), jnp.bfloat16)
    narrow = jax.ShapeDtypeStruct((count, slots, half), jnp.bfloat16)
    rows = SIDE * slots
    return pl.pallas_call(
        expert_kernel,
        grid=(count,),
        out_shape=[wide, wide, wide, narrow, narrow],
        in_specs=[
            pl.BlockSpec(memory_space=pltpu.SMEM),
            pl.BlockSpec((2, width), lambda i: (0, 0)),
            whole,
            whole,
            whole,
            split,
            split,
        ]
        + [any_space] * 6,
        out_specs=[whole, whole, whole, split, split],
        scratch_shapes=[
            pltpu.VMEM((2, half, units), jnp.bfloat16),
            pltpu.VMEM((2, half, units), jnp.bfloat16),
            pltpu.VMEM((2, units, half), jnp.bfloat16),
            pltpu.VMEM((rows, units), jnp.float32),
            pltpu.VMEM((rows, units), jnp.float32),
            pltpu.SemaphoreType.DMA((12,)),
        ],
        compiler_params=pltpu.CompilerParams(vmem_limit_bytes=VMEM_LIMIT),
        cost_estimate=pl.CostEstimate(
            flops=count * rows * width * units * 6,
            bytes_accessed=width * units * 6 + count * rows * width * 4,
            transcendentals=count * rows * units,
        ),
        name="expert_units",
    )(dp_index, modulation, own, left, right, far_a, far_b, *weights)


def combine_kernel(
    y_ref, ids_ref, dropped_ref, tokens_ref, normed_ref, mod_ref, router_ref, *refs
):
    back_refs, out_ref = refs[:-1], refs[-1]
    rows, width = tokens_ref.shape
    hidden_in = (
        normed_ref[...].astype(jnp.float32) * (1.0 + mod_ref[0:1, :]) + mod_ref[1:2, :]
    ).astype(jnp.bfloat16)
    gates = jax.nn.sigmoid(
        jnp.dot(hidden_in, router_ref[...], preferred_element_type=jnp.float32)
    )
    row = lax.broadcasted_iota(jnp.int32, (rows, rows), 0)
    column = lax.broadcasted_iota(jnp.int32, (rows, rows), 1)
    before = (column < row).astype(jnp.bfloat16)
    lane = lax.broadcasted_iota(jnp.int32, (rows, SLOTS), 1)
    experts = lax.broadcasted_iota(jnp.int32, gates.shape, 1)
    kept = 1.0 - dropped_ref[...].astype(jnp.float32)
    picks, scales = [], []
    for offset in OFFSETS:
        expert = lax.rem(y_ref[0] + offset + SIDE, SIDE)
        match = (ids_ref[...] == expert).astype(jnp.float32)
        named = jnp.max(match, axis=1, keepdims=True)
        weight = jnp.sum(match * kept, axis=1, keepdims=True) * jnp.sum(
            jnp.where(experts == expert, gates, 0.0), axis=1, keepdims=True
        )
        rank = jnp.dot(
            before,
            jnp.broadcast_to(named, (rows, 128)).astype(jnp.bfloat16),
            preferred_element_type=jnp.float32,
        )[:, 0:1].astype(jnp.int32)
        picks.append(jnp.where((lane == rank) & (named > 0.0), 1.0, 0.0).astype(jnp.bfloat16))
        scales.append(weight)
    tile = width // 4
    for start in range(0, width, tile):
        total = tokens_ref[:, start : start + tile].astype(jnp.float32)
        for pick, weight, back_ref in zip(picks, scales, back_refs):
            total = total + weight * jnp.dot(
                pick, back_ref[:, start : start + tile], preferred_element_type=jnp.float32
            )
        out_ref[:, start : start + tile] = total.astype(jnp.bfloat16)


def combine(y_index, ids, dropped, tokens, normed, modulation, router, backs):
    rows, width = tokens.shape
    vmem = pl.BlockSpec(memory_space=pltpu.VMEM)
    return pl.pallas_call(
        combine_kernel,
        out_shape=jax.ShapeDtypeStruct((rows, width), jnp.bfloat16),
        in_specs=[pl.BlockSpec(memory_space=pltpu.SMEM)] + [vmem] * (6 + len(backs)),
        out_specs=vmem,
        compiler_params=pltpu.CompilerParams(vmem_limit_bytes=VMEM_LIMIT),
        cost_estimate=pl.CostEstimate(
            flops=2 * 4 * SLOTS * rows * width, bytes_accessed=10 * rows * width, transcendentals=0
        ),
        name="weigh_and_add",
    )(y_index, ids, dropped, tokens, normed, modulation, router, *backs)


def on_device(
    tokens,
    text_states,
    text_lengths,
    mod_weight,
    router_weight,
    gate_weight,
    up_weight,
    down_weight,
    expert_ids,
    dropped,
):
    _, rows, width = tokens.shape
    half = width // 2
    tokens = tokens[0]
    ids = expert_ids[0]
    y_index = (lax.axis_index("expert") // SIDE).astype(jnp.int32).reshape(1)
    dp_index = lax.axis_index("dp").astype(jnp.int32).reshape(1)

    normed, *bins = make_bins(y_index, ids.T, tokens)
    bins = dict(zip(OFFSETS, bins))

    swap = [(0, 1), (1, 0)]
    weights = []
    for own in (gate_weight, up_weight, down_weight):
        weights += [own, lax.ppermute(own, "dp", swap)]

    positions = jnp.arange(text_states.shape[1], dtype=jnp.int32)
    valid = (positions[None, :] < text_lengths[:, None]).astype(jnp.bfloat16)
    pooled = jnp.einsum("it,itc->ic", valid, text_states, preferred_element_type=jnp.float32)
    pooled = (pooled / text_lengths.astype(jnp.float32)[:, None]).astype(jnp.bfloat16)
    partial_value = jnp.dot(pooled, mod_weight, preferred_element_type=jnp.float32)
    spread = lax.all_to_all(partial_value, "seq", split_axis=0, concat_axis=0, tiled=True)
    columns = jnp.sum(spread, axis=0, keepdims=True)
    owners = lax.axis_size("expert")
    modulation = lax.all_to_all(
        jnp.broadcast_to(columns, (owners, columns.shape[1])),
        "expert",
        split_axis=0,
        concat_axis=0,
        tiled=True,
    ).reshape(2, width)

    arrived = {
        offset: bins[offset] if offset == 0 else shift(bins[offset], along_y(offset))
        for offset in OFFSETS
    }
    backs = {}
    for chunk in CHUNKS:
        own = jnp.stack([arrived[offset] for offset in chunk])
        left = shift(own, along_x(1))
        right = shift(own, along_x(-1))
        far_a = shift(left[:, :, :half], along_x(1))
        far_b = shift(right[:, :, half:], along_x(-1))
        out_own, out_left, out_right, out_far_a, out_far_b = run_expert(
            dp_index, modulation, own, left, right, far_a, far_b, weights
        )
        got_a = shift(out_far_a, along_x(-1))
        got_b = shift(out_far_b, along_x(1))
        out_left = jnp.concatenate([out_left[:, :, :half] + got_a, out_left[:, :, half:]], axis=2)
        out_right = jnp.concatenate(
            [out_right[:, :, :half], out_right[:, :, half:] + got_b], axis=2
        )
        from_right = shift(out_left, along_x(-1))
        from_left = shift(out_right, along_x(1))
        summed = (
            out_own.astype(jnp.float32)
            + from_right.astype(jnp.float32)
            + from_left.astype(jnp.float32)
        ).astype(jnp.bfloat16)
        for place, offset in enumerate(chunk):
            piece = summed[place]
            backs[offset] = piece if offset == 0 else shift(piece, along_y(-offset))
    result = combine(
        y_index,
        ids,
        dropped[0],
        tokens,
        normed,
        modulation,
        router_weight,
        [backs[offset] for offset in OFFSETS],
    )
    return result[None]


def solution(mesh):
    return jax.shard_map(
        on_device,
        mesh=mesh,
        in_specs=(
            P(("dp", "seq"), "expert", None),
            P("dp", None, "seq"),
            P("dp"),
            P("seq", "expert"),
            P(),
            P("dp", "expert"),
            P("dp", "expert"),
            P("expert", "dp"),
            P(("dp", "seq"), "expert", None),
            P(("dp", "seq"), "expert", None),
        ),
        out_specs=P(("dp", "seq"), "expert", None),
        check_vma=False,
    )
```

```python
import functools

import jax
import jax.numpy as jnp
from jax import lax
from jax.experimental import pallas as pl
from jax.experimental.pallas import tpu as pltpu
from jax.sharding import PartitionSpec as P

SIDE = 4
SLOTS = 72
OFFSETS = (0, 1, -1, 2)
BAND = 256
VMEM_LIMIT = 56 * 1024 * 1024
TRANSPOSED = (((1,), (1,)), ((), ()))


def along_x(step):
    return [
        (y * SIDE + x, y * SIDE + (x + step) % SIDE) for y in range(SIDE) for x in range(SIDE)
    ]


def along_y(step):
    return [
        (y * SIDE + x, ((y + step) % SIDE) * SIDE + x) for y in range(SIDE) for x in range(SIDE)
    ]


def shift(value, perm):
    return lax.ppermute(value, "expert", perm)


def after(value, *others):
    return lax.optimization_barrier((value,) + others)[0]


def bands(units):
    return [(start, min(BAND, units - start)) for start in range(0, units, BAND)]


def in_vmem():
    return pl.BlockSpec(memory_space=pltpu.VMEM)


def in_smem():
    return pl.BlockSpec(memory_space=pltpu.SMEM)


def bin_kernel(y_ref, ids_ref, tokens_ref, normed_ref, *bin_refs):
    rows, width = tokens_ref.shape
    for start in range(0, rows, 16):
        block = tokens_ref[start : start + 16, :].astype(jnp.float32)
        centre = jnp.sum(block, axis=1, keepdims=True) * (1.0 / width)
        block = block - centre
        spread = jnp.sum(block * block, axis=1, keepdims=True) * (1.0 / width)
        normed_ref[start : start + 16, :] = (block * lax.rsqrt(spread + 1e-06)).astype(
            jnp.bfloat16
        )
    before = (
        lax.broadcasted_iota(jnp.int32, (rows, rows), 0)
        < lax.broadcasted_iota(jnp.int32, (rows, rows), 1)
    ).astype(jnp.bfloat16)
    place = lax.broadcasted_iota(jnp.int32, (8, rows), 0)
    expert = jnp.full((8, rows), -1, jnp.int32)
    for k, offset in enumerate(OFFSETS):
        expert = jnp.where(place == k, lax.rem(y_ref[0] + offset + SIDE, SIDE), expert)
    named = jnp.where((ids_ref[0:1, :] == expert) | (ids_ref[1:2, :] == expert), 1.0, 0.0)
    rank = jnp.dot(named.astype(jnp.bfloat16), before, preferred_element_type=jnp.float32)
    rank = jnp.where(named > 0.0, rank, -1.0)
    slot = lax.broadcasted_iota(jnp.int32, (SLOTS, rows), 0).astype(jnp.float32)
    normed = normed_ref[...]
    for k, bin_ref in enumerate(bin_refs):
        pick = jnp.where(slot == rank[k : k + 1, :], 1.0, 0.0).astype(jnp.bfloat16)
        bin_ref[...] = jnp.dot(pick, normed, preferred_element_type=jnp.float32).astype(
            jnp.bfloat16
        )


def make_bins(y_index, ids_rows, tokens):
    rows, width = tokens.shape
    return pl.pallas_call(
        bin_kernel,
        out_shape=[jax.ShapeDtypeStruct((rows, width), jnp.bfloat16)]
        + [jax.ShapeDtypeStruct((SLOTS, width), jnp.bfloat16)] * len(OFFSETS),
        in_specs=[in_smem(), in_vmem(), in_vmem()],
        out_specs=[in_vmem()] * (1 + len(OFFSETS)),
        compiler_params=pltpu.CompilerParams(vmem_limit_bytes=VMEM_LIMIT),
        cost_estimate=pl.CostEstimate(
            flops=2 * 4 * SLOTS * rows * width, bytes_accessed=8 * rows * width, transcendentals=0
        ),
        name="normalise_and_bin",
    )(y_index, ids_rows, tokens)


def expert_kernel(
    in_pieces,
    dp_ref,
    mod_ref,
    own_ref,
    left_ref,
    right_ref,
    *refs,
):
    w_in, w_down, hidden_in, hidden, sems = refs[-5:]
    refs = refs[:-5]
    far_refs, refs = refs[:in_pieces], refs[in_pieces:]
    gate_own, gate_far, up_own, up_far, down_own, down_far = refs[:6]
    out_own, out_left, out_right, *out_fars = refs[6:]
    size, width = own_ref.shape
    half = width // 2
    units = gate_own.shape[0]
    dp = dp_ref[0]
    spans = bands(units)
    tasks = []
    for number, (start, count) in enumerate(spans):
        for bank in range(2):
            for place, (own, far) in enumerate(((gate_own, gate_far), (up_own, up_far))):
                target = w_in.at[bank, pl.ds(2 * start + place * count, count)]
                span = pl.ds(start, count)
                tasks.append((own.at[span], far.at[span], target, number, bank))
    for bank in range(2):
        tasks.append((down_own, down_far, w_down.at[bank], len(spans) + bank, bank))
    for own, far, target, sem, bank in tasks:

        @pl.when(dp == bank)
        def _(own=own, target=target, sem=sem):
            pltpu.make_async_copy(own, target, sems.at[sem]).start()

        @pl.when(dp != bank)
        def _(far=far, target=target, sem=sem):
            pltpu.make_async_copy(far, target, sems.at[sem]).start()

    def wait(number):
        for own, _, target, sem, _ in tasks:
            if sem == number:
                pltpu.make_async_copy(own, target, sems.at[sem]).wait()

    for start in range(0, width, BAND):
        span = slice(start, start + BAND)
        piece, column = divmod(start, width // in_pieces)
        far_block = far_refs[piece][:, column : column + BAND]
        values = jnp.concatenate(
            [
                block.astype(jnp.float32)
                for block in (own_ref[:, span], left_ref[:, span], right_ref[:, span], far_block)
            ],
            axis=0,
        )
        hidden_in[:, span] = (values * (1.0 + mod_ref[0:1, span]) + mod_ref[1:2, span]).astype(
            jnp.bfloat16
        )
    for number, (start, count) in enumerate(spans):
        wait(number)
        both = 0.0
        for bank in range(2):
            both = both + lax.dot_general(
                hidden_in[:, bank * half : (bank + 1) * half],
                w_in[bank, 2 * start : 2 * (start + count), :],
                TRANSPOSED,
                preferred_element_type=jnp.float32,
            )
        hidden[:, start : start + count] = (
            jax.nn.silu(both[:, :count]) * both[:, count:]
        ).astype(jnp.bfloat16)
    tile = half // 2
    for start in range(0, width, tile):
        bank = start // half
        if start % half == 0:
            wait(len(spans) + bank)
        span = slice(start, start + tile)
        column = start % half
        out = jnp.dot(
            hidden[...],
            w_down[bank, :, column : column + tile],
            preferred_element_type=jnp.float32,
        )
        out_own[:, span] = out[0:size].astype(jnp.bfloat16)
        out_left[:, span] = out[size : 2 * size].astype(jnp.bfloat16)
        out_right[:, span] = out[2 * size : 3 * size].astype(jnp.bfloat16)
        piece, column = divmod(start, width // len(out_fars))
        out_fars[piece][:, column : column + tile] = out[3 * size : 4 * size].astype(
            jnp.bfloat16
        )


def run_expert(dp_index, modulation, own, left, right, fars, weights, pieces):
    size, width = own.shape
    half = width // 2
    units = weights[0].shape[0]
    wide = jax.ShapeDtypeStruct((size, width), jnp.bfloat16)
    narrow = jax.ShapeDtypeStruct((size, width // pieces), jnp.bfloat16)
    rows = SIDE * size
    return pl.pallas_call(
        functools.partial(expert_kernel, len(fars)),
        out_shape=[wide] * 3 + [narrow] * pieces,
        in_specs=[in_smem()]
        + [in_vmem()] * (4 + len(fars))
        + [pl.BlockSpec(memory_space=pl.ANY)] * len(weights),
        out_specs=[in_vmem()] * (3 + pieces),
        scratch_shapes=[
            pltpu.VMEM((2, 2 * units, half), jnp.bfloat16),
            pltpu.VMEM((2, units, half), jnp.bfloat16),
            pltpu.VMEM((rows, width), jnp.bfloat16),
            pltpu.VMEM((rows, units), jnp.bfloat16),
            pltpu.SemaphoreType.DMA((len(bands(units)) + 2,)),
        ],
        compiler_params=pltpu.CompilerParams(vmem_limit_bytes=VMEM_LIMIT),
        cost_estimate=pl.CostEstimate(
            flops=rows * width * units * 12,
            bytes_accessed=width * units * 6 + rows * width * 4,
            transcendentals=rows * units,
        ),
        name="expert_units",
    )(dp_index, modulation, own, left, right, *fars, *weights)


def weigh_kernel(y_ref, ids_ref, dropped_ref, normed_ref, mod_ref, router_ref, weight_ref, rank_ref):
    rows, _ = normed_ref.shape
    hidden_in = (
        normed_ref[...].astype(jnp.float32) * (1.0 + mod_ref[0:1, :]) + mod_ref[1:2, :]
    ).astype(jnp.bfloat16)
    gates = jax.nn.sigmoid(
        lax.dot_general(
            hidden_in, router_ref[...], TRANSPOSED, preferred_element_type=jnp.float32
        )
    )
    row = lax.broadcasted_iota(jnp.int32, (rows, rows), 0)
    column = lax.broadcasted_iota(jnp.int32, (rows, rows), 1)
    before = (column < row).astype(jnp.bfloat16)
    expert = lax.broadcasted_iota(jnp.int32, gates.shape, 1)
    weight = jnp.zeros(gates.shape, jnp.float32)
    named = jnp.zeros(gates.shape, jnp.float32)
    for k in range(2):
        chosen = ids_ref[:, k : k + 1] == expert
        kept = 1.0 - dropped_ref[:, k : k + 1].astype(jnp.float32)
        weight = weight + jnp.where(chosen, gates * kept, 0.0)
        named = named + jnp.where(chosen, 1.0, 0.0)
    rank = jnp.dot(before, named.astype(jnp.bfloat16), preferred_element_type=jnp.float32)
    rank = jnp.where(named > 0.0, rank, -1.0)
    for k, offset in enumerate(OFFSETS):
        here = expert == lax.rem(y_ref[0] + offset + SIDE, SIDE)
        weight_ref[:, k : k + 1] = jnp.sum(jnp.where(here, weight, 0.0), axis=1, keepdims=True)
        rank_ref[:, k : k + 1] = jnp.sum(jnp.where(here, rank, 0.0), axis=1, keepdims=True)


def weigh(y_index, ids, dropped, normed, modulation, router):
    rows, width = normed.shape
    return pl.pallas_call(
        weigh_kernel,
        out_shape=[jax.ShapeDtypeStruct((rows, 128), jnp.float32)] * 2,
        in_specs=[in_smem()] + [in_vmem()] * 5,
        out_specs=[in_vmem()] * 2,
        compiler_params=pltpu.CompilerParams(vmem_limit_bytes=VMEM_LIMIT),
        cost_estimate=pl.CostEstimate(
            flops=2 * 128 * rows * width, bytes_accessed=4 * rows * width, transcendentals=0
        ),
        name="weigh",
    )(y_index, ids, dropped, normed, modulation, router)


def combine_kernel(offsets, weight_ref, rank_ref, total_ref, *refs):
    back_refs, out_ref = refs[:-1], refs[-1]
    rows, width = out_ref.shape
    lane = lax.broadcasted_iota(jnp.int32, (rows, SLOTS), 1).astype(jnp.float32)
    tile = width // 4
    for start in range(0, width, tile):
        span = slice(start, start + tile)
        total = total_ref[:, span].astype(jnp.float32)
        for offset, group in zip(offsets, back_refs):
            k = OFFSETS.index(offset)
            pick = jnp.where(lane == rank_ref[:, k : k + 1], 1.0, 0.0).astype(jnp.bfloat16)
            total = total + weight_ref[:, k : k + 1] * jnp.dot(
                pick, group[:, span], preferred_element_type=jnp.float32
            )
        out_ref[:, span] = total.astype(out_ref.dtype)


def combine(offsets, weight, rank, total, backs, out_type):
    rows, width = total.shape
    return pl.pallas_call(
        functools.partial(combine_kernel, offsets),
        out_shape=jax.ShapeDtypeStruct((rows, width), out_type),
        in_specs=[in_vmem()] * (3 + len(backs)),
        out_specs=in_vmem(),
        compiler_params=pltpu.CompilerParams(vmem_limit_bytes=VMEM_LIMIT),
        cost_estimate=pl.CostEstimate(
            flops=2 * len(backs) * SLOTS * rows * width,
            bytes_accessed=10 * rows * width,
            transcendentals=0,
        ),
        name="add_terms",
    )(weight, rank, total, *backs)


def on_device(
    tokens,
    text_states,
    text_lengths,
    mod_weight,
    router_weight,
    gate_weight,
    up_weight,
    down_weight,
    expert_ids,
    dropped,
):
    _, rows, width = tokens.shape
    half = width // 2
    tokens = tokens[0]
    ids = expert_ids[0]
    owners = lax.axis_size("expert")
    y_index = (lax.axis_index("expert") // SIDE).astype(jnp.int32).reshape(1)
    dp_index = lax.axis_index("dp").astype(jnp.int32).reshape(1)

    def exchange(value, axis="expert"):
        return lax.all_to_all(value, axis, split_axis=0, concat_axis=0, tiled=True)

    swap = [(0, 1), (1, 0)]
    weights = []
    for own in (gate_weight.T, up_weight.T, down_weight):
        weights += [own, lax.ppermute(own, "dp", swap)]

    normed, *bins = make_bins(y_index, ids.T, tokens)
    bins = dict(zip(OFFSETS, bins))

    positions = jnp.arange(text_states.shape[1], dtype=jnp.int32)
    valid = (positions[None, :] < text_lengths[:, None]).astype(jnp.bfloat16)
    pooled = jnp.einsum("it,itc->ic", valid, text_states, preferred_element_type=jnp.float32)
    pooled = (pooled / text_lengths.astype(jnp.float32)[:, None]).astype(jnp.bfloat16)
    partial_value = jnp.dot(pooled, mod_weight, preferred_element_type=jnp.float32)
    router = jnp.pad(router_weight.T, ((0, 128 - SIDE), (0, 0)))

    arrived = {offset: shift(bins[offset], along_y(offset)) for offset in (1, -1)}
    swapped = weights[1::2]
    start = after(bins[0], *swapped)
    arrived[2] = shift(after(bins[2], *swapped), along_y(2))
    sides, across, middle = (1, -1), (2,), (0,)
    sent = {sides: jnp.concatenate([arrived[1], arrived[-1]], axis=0), middle: start}
    near = {
        chunk: (shift(sent[chunk], along_x(1)), shift(sent[chunk], along_x(-1)))
        for chunk in (middle, sides)
    }
    partial_value = after(partial_value, sent[sides], *swapped)
    columns = jnp.sum(exchange(partial_value, "seq"), axis=0, keepdims=True)
    modulation = exchange(jnp.broadcast_to(columns, (owners, columns.shape[1]))).reshape(2, width)
    left, right = (after(value, columns) for value in near[sides])
    far = {sides: (shift(left[:, :half], along_x(1)), shift(right[:, half:], along_x(-1)))}
    sent[across] = after(arrived[2], *far[sides])
    near[across] = shift(sent[across], along_x(1)), shift(sent[across], along_x(-1))
    far[across] = (shift(sent[across], along_x(2)),)

    weight, rank = weigh(y_index, ids, dropped[0], normed, modulation, router)
    backs = {}
    for chunk in (sides, across, middle):
        pieces = 1 if chunk == middle else 2
        out_own, out_left, out_right, *out_fars = run_expert(
            dp_index, modulation, sent[chunk], *near[chunk], far[chunk], weights, pieces
        )
        modulation = after(modulation, out_fars[0])
        if chunk == sides:
            far[middle] = (shift(after(bins[0], out_fars[0]), along_x(2)),)
        parts = [out_own]
        if pieces == 1:
            parts.append(shift(out_fars[0], along_x(2)))
        else:
            got_a = shift(out_fars[0], along_x(-1))
            got_b = shift(out_fars[1], along_x(1))
            out_left = jnp.concatenate([out_left[:, :half] + got_a, out_left[:, half:]], axis=1)
            out_right = jnp.concatenate(
                [out_right[:, :half], out_right[:, half:] + got_b], axis=1
            )
        parts += [shift(out_left, along_x(-1)), shift(out_right, along_x(1))]
        summed = sum(part.astype(jnp.float32) for part in parts).astype(jnp.bfloat16)
        for k, offset in enumerate(chunk):
            piece = summed[k * SLOTS : (k + 1) * SLOTS]
            backs[offset] = piece if offset == 0 else shift(piece, along_y(-offset))
    total = combine(
        OFFSETS, weight, rank, tokens, [backs[offset] for offset in OFFSETS], jnp.bfloat16
    )
    return total[None]


def solution(mesh):
    return jax.shard_map(
        on_device,
        mesh=mesh,
        in_specs=(
            P(("dp", "seq"), "expert", None),
            P("dp", None, "seq"),
            P("dp"),
            P("seq", "expert"),
            P(),
            P("dp", "expert"),
            P("dp", "expert"),
            P("expert", "dp"),
            P(("dp", "seq"), "expert", None),
            P(("dp", "seq"), "expert", None),
        ),
        out_specs=P(("dp", "seq"), "expert", None),
        check_vma=False,
    )
```

```python
import functools

import jax
import jax.numpy as jnp
from jax import lax
from jax.experimental import pallas as pl
from jax.experimental.pallas import tpu as pltpu
from jax.sharding import PartitionSpec as P

SIDE = 4
SLOTS = 72
MOST = 68
OFFSETS = (0, 1, -1, 2)
BAND = 256
VMEM_LIMIT = 20 * 1024 * 1024
TRANSPOSED = (((1,), (1,)), ((), ()))


def along_x(step):
    return [
        (y * SIDE + x, y * SIDE + (x + step) % SIDE) for y in range(SIDE) for x in range(SIDE)
    ]


def along_y(step):
    return [
        (y * SIDE + x, ((y + step) % SIDE) * SIDE + x) for y in range(SIDE) for x in range(SIDE)
    ]


def shift(value, perm):
    return lax.ppermute(value, "expert", perm)


def after(value, *others):
    return lax.optimization_barrier((value,) + others)[0]


def bands(units):
    return [(start, min(BAND, units - start)) for start in range(0, units, BAND)]


def in_vmem():
    return pl.BlockSpec(memory_space=pltpu.VMEM)


def in_smem():
    return pl.BlockSpec(memory_space=pltpu.SMEM)


def ranks(y_ref, ids_ref):
    rows = ids_ref.shape[1]
    before = (
        lax.broadcasted_iota(jnp.int32, (rows, rows), 0)
        < lax.broadcasted_iota(jnp.int32, (rows, rows), 1)
    ).astype(jnp.bfloat16)
    place = lax.broadcasted_iota(jnp.int32, (8, rows), 0)
    expert = jnp.full((8, rows), -1, jnp.int32)
    for k, offset in enumerate(OFFSETS):
        expert = jnp.where(place == k, lax.rem(y_ref[0] + offset + SIDE, SIDE), expert)
    named = jnp.where((ids_ref[0:1, :] == expert) | (ids_ref[1:2, :] == expert), 1.0, 0.0)
    rank = jnp.dot(named.astype(jnp.bfloat16), before, preferred_element_type=jnp.float32)
    return jnp.where(named > 0.0, rank, -1.0)


def bin_kernel(y_ref, ids_ref, tokens_ref, normed_ref, *bin_refs):
    rows, width = tokens_ref.shape
    for start in range(0, rows, 16):
        block = tokens_ref[start : start + 16, :].astype(jnp.float32)
        centre = jnp.sum(block, axis=1, keepdims=True) * (1.0 / width)
        block = block - centre
        spread = jnp.sum(block * block, axis=1, keepdims=True) * (1.0 / width)
        normed_ref[start : start + 16, :] = (block * lax.rsqrt(spread + 1e-06)).astype(
            jnp.bfloat16
        )
    rank = ranks(y_ref, ids_ref)
    slot = lax.broadcasted_iota(jnp.int32, (SLOTS, rows), 0).astype(jnp.float32)
    normed = normed_ref[...]
    for k, bin_ref in enumerate(bin_refs):
        pick = jnp.where(slot == rank[k : k + 1, :], 1.0, 0.0).astype(jnp.bfloat16)
        for half in range(2):
            span = slice(half * (width // 2), (half + 1) * (width // 2))
            bin_ref[half] = jnp.dot(
                pick, normed[:, span], preferred_element_type=jnp.float32
            ).astype(jnp.bfloat16)


def make_bins(y_index, ids_rows, tokens):
    rows, width = tokens.shape
    return pl.pallas_call(
        bin_kernel,
        out_shape=[jax.ShapeDtypeStruct((rows, width), jnp.bfloat16)]
        + [jax.ShapeDtypeStruct((2, SLOTS, width // 2), jnp.bfloat16)] * len(OFFSETS),
        in_specs=[in_smem(), in_vmem(), in_vmem()],
        out_specs=[in_vmem()] * (1 + len(OFFSETS)),
        compiler_params=pltpu.CompilerParams(vmem_limit_bytes=VMEM_LIMIT),
        cost_estimate=pl.CostEstimate(
            flops=2 * 4 * SLOTS * rows * width, bytes_accessed=8 * rows * width, transcendentals=0
        ),
        name="normalise_and_bin",
    )(y_index, ids_rows, tokens)


def pack_kernel(first_ref, second_ref, out_ref):
    row = lax.broadcasted_iota(jnp.int32, (2 * MOST, SLOTS), 0)
    column = lax.broadcasted_iota(jnp.int32, (2 * MOST, SLOTS), 1)
    first = ((row == column) & (row < MOST)).astype(jnp.bfloat16)
    second = (row == column + MOST).astype(jnp.bfloat16)
    for side in range(2):
        out_ref[side] = (
            jnp.dot(first, first_ref[side], preferred_element_type=jnp.float32)
            + jnp.dot(second, second_ref[side], preferred_element_type=jnp.float32)
        ).astype(jnp.bfloat16)


def pack(first, second):
    _, slots, half = first.shape
    return pl.pallas_call(
        pack_kernel,
        out_shape=jax.ShapeDtypeStruct((2, 2 * MOST, half), jnp.bfloat16),
        in_specs=[in_vmem()] * 2,
        out_specs=in_vmem(),
        compiler_params=pltpu.CompilerParams(vmem_limit_bytes=VMEM_LIMIT),
        cost_estimate=pl.CostEstimate(
            flops=16 * MOST * slots * half, bytes_accessed=16 * MOST * half, transcendentals=0
        ),
        name="pack",
    )(first, second)


def expert_kernel(
    dp_ref,
    mod_ref,
    own_ref,
    left_ref,
    right_ref,
    *refs,
):
    *far_refs, gate_own, gate_far, up_own, up_far, down_own, down_far = refs[:-6]
    out_own, out_left, out_right, out_far, hidden_in, hidden = refs[-6:]
    _, size, half = own_ref.shape
    units = gate_own.shape[0]
    banks = (dp_ref[0], 1 - dp_ref[0])
    for side in range(2):
        far_ref = far_refs[side] if len(far_refs) == 2 else far_refs[0].at[side]
        for start in range(0, half, BAND):
            span = slice(start, start + BAND)
            column = slice(side * half + start, side * half + start + BAND)
            blocks = [ref[side, :, span] for ref in (own_ref, left_ref, right_ref)]
            values = jnp.concatenate(
                [block.astype(jnp.float32) for block in blocks + [far_ref[:, span]]], axis=0
            )
            hidden_in[banks[side], :, span] = (
                values * (1.0 + mod_ref[0:1, column]) + mod_ref[1:2, column]
            ).astype(jnp.bfloat16)
    for start, count in bands(units):
        span = slice(start, start + count)
        both = 0.0
        for bank, (gate, up) in enumerate(((gate_own, up_own), (gate_far, up_far))):
            both = both + lax.dot_general(
                hidden_in[bank],
                jnp.concatenate([gate[span, :], up[span, :]], axis=0),
                TRANSPOSED,
                preferred_element_type=jnp.float32,
            )
        hidden[:, span] = (jax.nn.silu(both[:, :count]) * both[:, count:]).astype(jnp.bfloat16)
    tile = half // 2
    outs = (out_own, out_left, out_right, out_far)
    for bank, down in enumerate((down_own, down_far)):
        for start in range(0, half, tile):
            span = slice(start, start + tile)
            out = jnp.dot(hidden[...], down[:, span], preferred_element_type=jnp.float32)
            for k, out_ref in enumerate(outs):
                out_ref[banks[bank], :, span] = out[k * size : (k + 1) * size].astype(
                    jnp.bfloat16
                )


def run_expert(dp_index, modulation, own, left, right, fars, weights):
    _, size, half = own.shape
    units = weights[0].shape[0]
    rows = SIDE * size
    return pl.pallas_call(
        expert_kernel,
        out_shape=[jax.ShapeDtypeStruct(own.shape, jnp.bfloat16)] * 4,
        in_specs=[in_smem()] + [in_vmem()] * (4 + len(fars) + len(weights)),
        out_specs=[in_vmem()] * 4,
        scratch_shapes=[
            pltpu.VMEM((2, rows, half), jnp.bfloat16),
            pltpu.VMEM((rows, units), jnp.bfloat16),
        ],
        compiler_params=pltpu.CompilerParams(vmem_limit_bytes=VMEM_LIMIT),
        cost_estimate=pl.CostEstimate(
            flops=rows * half * units * 24,
            bytes_accessed=half * units * 12 + rows * half * 8,
            transcendentals=rows * units,
        ),
        name="expert_units",
    )(dp_index, modulation, own, left, right, *fars, *weights)


def weigh_kernel(y_ref, ids_ref, dropped_ref, normed_ref, mod_ref, router_ref, weight_ref, rank_ref):
    rows, _ = normed_ref.shape
    hidden_in = (
        normed_ref[...].astype(jnp.float32) * (1.0 + mod_ref[0:1, :]) + mod_ref[1:2, :]
    ).astype(jnp.bfloat16)
    gates = jax.nn.sigmoid(
        lax.dot_general(
            router_ref[...], hidden_in, TRANSPOSED, preferred_element_type=jnp.float32
        )
    )
    which = lax.broadcasted_iota(jnp.int32, gates.shape, 0)
    weights = []
    for offset in OFFSETS:
        expert = lax.rem(y_ref[0] + offset + SIDE, SIDE)
        gate = jnp.sum(jnp.where(which == expert, gates, 0.0), axis=0, keepdims=True)
        kept = jnp.zeros((1, rows), jnp.float32)
        for k in range(2):
            chosen = jnp.where(ids_ref[k : k + 1, :] == expert, 1.0, 0.0)
            kept = kept + chosen * (1.0 - dropped_ref[k : k + 1, :].astype(jnp.float32))
        weights.append(gate * kept)
    weight_ref[...] = jnp.concatenate(weights + weights, axis=0)
    rank_ref[...] = ranks(y_ref, ids_ref)


def weigh(y_index, ids, dropped, normed, modulation, router):
    rows, width = normed.shape
    return pl.pallas_call(
        weigh_kernel,
        out_shape=[jax.ShapeDtypeStruct((8, rows), jnp.float32)] * 2,
        in_specs=[in_smem()] + [in_vmem()] * 5,
        out_specs=[in_vmem()] * 2,
        compiler_params=pltpu.CompilerParams(vmem_limit_bytes=VMEM_LIMIT),
        cost_estimate=pl.CostEstimate(
            flops=2 * 128 * rows * width, bytes_accessed=4 * rows * width, transcendentals=0
        ),
        name="weigh",
    )(y_index, ids, dropped, normed, modulation, router)


def combine_kernel(counts, weight_ref, rank_ref, total_ref, *refs):
    out_ref = refs[-1]
    rows, width = out_ref.shape
    picks, scales = [], []
    for k in range(len(counts)):
        slots = refs[sum(counts[:k])].shape[1]
        slot = lax.broadcasted_iota(jnp.int32, (slots, rows), 0).astype(jnp.float32)
        pick = jnp.where(slot == rank_ref[k : k + 1, :], 1.0, 0.0)
        scales.append(jnp.sum(pick * weight_ref[k : k + 1, :], axis=1, keepdims=True))
        picks.append(pick.astype(jnp.bfloat16))
    half = width // 2
    tile = half // 2
    for start in range(0, width, tile):
        span = slice(start, start + tile)
        side, column = start // half, slice(start % half, start % half + tile)
        total = total_ref[:, span].astype(jnp.float32)
        first = 0
        for pick, scale, count in zip(picks, scales, counts):
            back = sum(
                ref[side, :, column].astype(jnp.float32) for ref in refs[first : first + count]
            )
            first += count
            total = total + lax.dot_general(
                pick,
                (back * scale).astype(jnp.bfloat16),
                (((0,), (0,)), ((), ())),
                preferred_element_type=jnp.float32,
            )
        out_ref[:, span] = total.astype(out_ref.dtype)


def combine(weight, rank, tokens, backs):
    rows, width = tokens.shape
    counts = [len(group) for group in backs]
    return pl.pallas_call(
        functools.partial(combine_kernel, counts),
        out_shape=jax.ShapeDtypeStruct((rows, width), jnp.bfloat16),
        in_specs=[in_vmem()] * (3 + sum(counts)),
        out_specs=in_vmem(),
        compiler_params=pltpu.CompilerParams(vmem_limit_bytes=VMEM_LIMIT),
        cost_estimate=pl.CostEstimate(
            flops=2 * len(backs) * SLOTS * rows * width,
            bytes_accessed=10 * rows * width,
            transcendentals=0,
        ),
        name="add_terms",
    )(weight, rank, tokens, *sum(backs, []))


def on_device(
    tokens,
    text_states,
    text_lengths,
    mod_weight,
    router_weight,
    gate_weight,
    up_weight,
    down_weight,
    expert_ids,
    dropped,
):
    _, rows, width = tokens.shape
    tokens = tokens[0]
    ids = expert_ids[0].T
    owners = lax.axis_size("expert")
    y_index = (lax.axis_index("expert") // SIDE).astype(jnp.int32).reshape(1)
    dp_index = lax.axis_index("dp").astype(jnp.int32).reshape(1)

    def exchange(value, axis="expert"):
        return lax.all_to_all(value, axis, split_axis=0, concat_axis=0, tiled=True)

    normed, *bins = make_bins(y_index, ids, tokens)
    bins = dict(zip(OFFSETS, bins))

    positions = jnp.arange(text_states.shape[1], dtype=jnp.int32)
    valid = (positions[None, :] < text_lengths[:, None]).astype(jnp.bfloat16)
    pooled = jnp.einsum("it,itc->ic", valid, text_states, preferred_element_type=jnp.float32)
    pooled = (pooled / text_lengths.astype(jnp.float32)[:, None]).astype(jnp.bfloat16)
    partial_value = jnp.dot(pooled, mod_weight, preferred_element_type=jnp.float32)

    tie = lax.optimization_barrier
    left_of, right_of, across_x = along_x(-1), along_x(1), along_x(2)

    def both_ways(value):
        return shift(value, right_of), shift(value, left_of)

    def add_half(value, side, extra):
        halves = [value[0], value[1]]
        halves[side] = halves[side] + extra
        return jnp.stack(halves)

    def total_of(*parts):
        return sum(part.astype(jnp.float32) for part in parts).astype(jnp.bfloat16)

    def run(own, near, far):
        return run_expert(dp_index, modulation, own, *near, far, weights)

    middle = bins[0]
    from_up, from_down = shift(bins[1], along_y(1)), shift(bins[-1], along_y(-1))
    from_up, from_down, partial_value, *middle_near = tie(
        (from_up, from_down, partial_value, *both_ways(middle))
    )

    sides = pack(from_up, from_down)
    near = both_ways(sides)
    swap = [(0, 1), (1, 0)]
    owns = tie((gate_weight.T, up_weight.T, down_weight, from_up))[:3]
    swapped = [lax.ppermute(own, "dp", swap) for own in owns]
    columns = jnp.sum(exchange(partial_value, "seq"), axis=0, keepdims=True)
    columns, outer, *rest = tie((columns, bins[2], *near, *swapped))
    near, swapped = rest[:2], rest[2:]
    weights = [owns[0], swapped[0], owns[1], swapped[1], owns[2], swapped[2]]

    far = shift(near[0][0], right_of), shift(near[1][1], left_of)
    outer = shift(outer, along_y(2))
    modulation = exchange(jnp.broadcast_to(columns, (owners, columns.shape[1]))).reshape(2, width)
    modulation, outer, middle, *far = tie((modulation, outer, middle, *far))

    outer_near, outer_far = both_ways(outer), shift(outer, across_x)
    middle_far = shift(middle, across_x)
    out_sides = run(sides, near, far)
    middle_far, outer_far, *rest = tie((middle_far, outer_far, *outer_near, *out_sides))
    outer_near, out_sides = rest[:2], rest[2:]

    got = shift(out_sides[3][0], left_of), shift(out_sides[3][1], right_of)
    out_outer = run(outer, outer_near, (outer_far,))
    rest = tie((*got, *out_outer))
    got, out_outer = rest[:2], rest[2:]

    sums = (
        shift(add_half(out_sides[1], 0, got[0]), left_of),
        shift(add_half(out_sides[2], 1, got[1]), right_of),
    )
    got = shift(out_outer[3][0], left_of), shift(out_outer[3][1], right_of)
    out_middle = run(middle, middle_near, (middle_far,))
    rest = tie((*sums, *got, *out_middle))
    sums, got, out_middle = rest[:2], rest[2:4], rest[4:]

    outer_sums = (
        shift(add_half(out_outer[1], 0, got[0]), left_of),
        shift(add_half(out_outer[2], 1, got[1]), right_of),
    )
    back = total_of(out_sides[0], *sums)
    backs = {
        1: [shift(back[:, :MOST], along_y(-1))],
        -1: [shift(back[:, MOST:], along_y(1))],
    }
    middle_far = shift(out_middle[3], across_x)
    outer_back = total_of(out_outer[0], *outer_sums)
    to_left, to_right, outer_back = tie((out_middle[1], out_middle[2], outer_back))
    middle_sums = middle_far, shift(to_left, left_of), shift(to_right, right_of)
    weight, rank = weigh(y_index, ids, dropped[0].T, normed, modulation, router_weight.T)
    backs[2] = [shift(outer_back, along_y(2))]
    backs[0] = [out_middle[0], *middle_sums]
    total = combine(weight, rank, tokens, [backs[offset] for offset in OFFSETS])
    return total[None]


def solution(mesh):
    return jax.shard_map(
        on_device,
        mesh=mesh,
        in_specs=(
            P(("dp", "seq"), "expert", None),
            P("dp", None, "seq"),
            P("dp"),
            P("seq", "expert"),
            P(),
            P("dp", "expert"),
            P("dp", "expert"),
            P("expert", "dp"),
            P(("dp", "seq"), "expert", None),
            P(("dp", "seq"), "expert", None),
        ),
        out_specs=P(("dp", "seq"), "expert", None),
        check_vma=False,
    )
```

```python
import functools

import jax
import jax.numpy as jnp
from jax import lax
from jax.experimental import pallas as pl
from jax.experimental.pallas import tpu as pltpu
from jax.sharding import PartitionSpec as P

SIDE = 4
SLOTS = 72
MOST = 68
OFFSETS = (0, 1, -1, 2)
BAND = 256
VMEM_LIMIT = 20 * 1024 * 1024
TRANSPOSED = (((1,), (1,)), ((), ()))


def along_x(step):
    return [
        (y * SIDE + x, y * SIDE + (x + step) % SIDE) for y in range(SIDE) for x in range(SIDE)
    ]


def along_y(step):
    return [
        (y * SIDE + x, ((y + step) % SIDE) * SIDE + x) for y in range(SIDE) for x in range(SIDE)
    ]


def shift(value, perm):
    return lax.ppermute(value, "expert", perm)


def after(value, *others):
    return lax.optimization_barrier((value,) + others)[0]


def in_vmem():
    return pl.BlockSpec(memory_space=pltpu.VMEM)


def in_smem():
    return pl.BlockSpec(memory_space=pltpu.SMEM)


def ranks(y_ref, ids_ref):
    rows = ids_ref.shape[1]
    before = (
        lax.broadcasted_iota(jnp.int32, (rows, rows), 0)
        < lax.broadcasted_iota(jnp.int32, (rows, rows), 1)
    ).astype(jnp.bfloat16)
    place = lax.broadcasted_iota(jnp.int32, (8, rows), 0)
    expert = jnp.full((8, rows), -1, jnp.int32)
    for k, offset in enumerate(OFFSETS):
        expert = jnp.where(place == k, lax.rem(y_ref[0] + offset + SIDE, SIDE), expert)
    named = jnp.where((ids_ref[0:1, :] == expert) | (ids_ref[1:2, :] == expert), 1.0, 0.0)
    rank = jnp.dot(named.astype(jnp.bfloat16), before, preferred_element_type=jnp.float32)
    return jnp.where(named > 0.0, rank, -1.0)


def bin_kernel(y_ref, ids_ref, tokens_ref, normed_ref, *bin_refs):
    rows, width = tokens_ref.shape
    for start in range(0, rows, 16):
        block = tokens_ref[start : start + 16, :].astype(jnp.float32)
        centre = jnp.sum(block, axis=1, keepdims=True) * (1.0 / width)
        block = block - centre
        spread = jnp.sum(block * block, axis=1, keepdims=True) * (1.0 / width)
        normed_ref[start : start + 16, :] = (block * lax.rsqrt(spread + 1e-06)).astype(
            jnp.bfloat16
        )
    rank = ranks(y_ref, ids_ref)
    slot = lax.broadcasted_iota(jnp.int32, (SLOTS, rows), 0).astype(jnp.float32)
    normed = normed_ref[...]
    for k, bin_ref in enumerate(bin_refs):
        pick = jnp.where(slot == rank[k : k + 1, :], 1.0, 0.0).astype(jnp.bfloat16)
        for half in range(2):
            span = slice(half * (width // 2), (half + 1) * (width // 2))
            bin_ref[half] = jnp.dot(
                pick, normed[:, span], preferred_element_type=jnp.float32
            ).astype(jnp.bfloat16)


def make_bins(y_index, ids_rows, tokens):
    rows, width = tokens.shape
    return pl.pallas_call(
        bin_kernel,
        out_shape=[jax.ShapeDtypeStruct((rows, width), jnp.bfloat16)]
        + [jax.ShapeDtypeStruct((2, SLOTS, width // 2), jnp.bfloat16)] * len(OFFSETS),
        in_specs=[in_smem(), in_vmem(), in_vmem()],
        out_specs=[in_vmem()] * (1 + len(OFFSETS)),
        compiler_params=pltpu.CompilerParams(vmem_limit_bytes=VMEM_LIMIT),
        cost_estimate=pl.CostEstimate(
            flops=2 * 4 * SLOTS * rows * width, bytes_accessed=8 * rows * width, transcendentals=0
        ),
        name="normalise_and_bin",
    )(y_index, ids_rows, tokens)


def pack_kernel(first_ref, second_ref, out_ref):
    row = lax.broadcasted_iota(jnp.int32, (2 * MOST, SLOTS), 0)
    column = lax.broadcasted_iota(jnp.int32, (2 * MOST, SLOTS), 1)
    first = ((row == column) & (row < MOST)).astype(jnp.bfloat16)
    second = (row == column + MOST).astype(jnp.bfloat16)
    for side in range(2):
        out_ref[side] = (
            jnp.dot(first, first_ref[side], preferred_element_type=jnp.float32)
            + jnp.dot(second, second_ref[side], preferred_element_type=jnp.float32)
        ).astype(jnp.bfloat16)


def pack(first, second):
    _, slots, half = first.shape
    return pl.pallas_call(
        pack_kernel,
        out_shape=jax.ShapeDtypeStruct((2, 2 * MOST, half), jnp.bfloat16),
        in_specs=[in_vmem()] * 2,
        out_specs=in_vmem(),
        compiler_params=pltpu.CompilerParams(vmem_limit_bytes=VMEM_LIMIT),
        cost_estimate=pl.CostEstimate(
            flops=16 * MOST * slots * half, bytes_accessed=16 * MOST * half, transcendentals=0
        ),
        name="pack",
    )(first, second)


def expert_kernel(
    dp_ref,
    mod_ref,
    own_ref,
    left_ref,
    right_ref,
    *refs,
):
    *far_refs, gate_own, gate_far, up_own, up_far, down_own, down_far = refs[:-6]
    out_own, out_left, out_right, out_far, hidden_in, hidden = refs[-6:]
    _, size, half = own_ref.shape
    units = gate_own.shape[0]
    banks = (dp_ref[0], 1 - dp_ref[0])
    for side in range(2):
        far_ref = far_refs[side] if len(far_refs) == 2 else far_refs[0].at[side]

        def prepare(step, carry, side=side, far_ref=far_ref):
            start = pl.multiple_of(step * BAND, BAND)
            span = pl.ds(start, BAND)
            column = pl.ds(pl.multiple_of(side * half + start, BAND), BAND)
            blocks = [ref[side, :, span] for ref in (own_ref, left_ref, right_ref)]
            values = jnp.concatenate(
                [block.astype(jnp.float32) for block in blocks + [far_ref[:, span]]], axis=0
            )
            hidden_in[banks[side], :, span] = (
                values * (1.0 + mod_ref[0:1, column]) + mod_ref[1:2, column]
            ).astype(jnp.bfloat16)
            return carry

        lax.fori_loop(0, half // BAND, prepare, 0)

    def band(start, count):
        span = pl.ds(start, count)
        both = 0.0
        for bank, (gate, up) in enumerate(((gate_own, up_own), (gate_far, up_far))):
            both = both + lax.dot_general(
                hidden_in[bank],
                jnp.concatenate([gate[span, :], up[span, :]], axis=0),
                TRANSPOSED,
                preferred_element_type=jnp.float32,
            )
        hidden[:, span] = (jax.nn.silu(both[:, :count]) * both[:, count:]).astype(jnp.bfloat16)

    def full_band(step, carry):
        band(pl.multiple_of(step * BAND, BAND), BAND)
        return carry

    lax.fori_loop(0, units // BAND, full_band, 0)
    if units % BAND:
        band(units - units % BAND, units % BAND)
    tile = half // 2
    outs = (out_own, out_left, out_right, out_far)
    for bank, down in enumerate((down_own, down_far)):

        def project(step, carry, bank=bank, down=down):
            span = pl.ds(pl.multiple_of(step * tile, tile), tile)
            out = jnp.dot(hidden[...], down[:, span], preferred_element_type=jnp.float32)
            for k, out_ref in enumerate(outs):
                out_ref[banks[bank], :, span] = out[k * size : (k + 1) * size].astype(
                    jnp.bfloat16
                )
            return carry

        lax.fori_loop(0, half // tile, project, 0)


def run_expert(dp_index, modulation, own, left, right, fars, weights):
    _, size, half = own.shape
    units = weights[0].shape[0]
    rows = SIDE * size
    return pl.pallas_call(
        expert_kernel,
        out_shape=[jax.ShapeDtypeStruct(own.shape, jnp.bfloat16)] * 4,
        in_specs=[in_smem()] + [in_vmem()] * (4 + len(fars) + len(weights)),
        out_specs=[in_vmem()] * 4,
        scratch_shapes=[
            pltpu.VMEM((2, rows, half), jnp.bfloat16),
            pltpu.VMEM((rows, units), jnp.bfloat16),
        ],
        compiler_params=pltpu.CompilerParams(vmem_limit_bytes=VMEM_LIMIT),
        cost_estimate=pl.CostEstimate(
            flops=rows * half * units * 24,
            bytes_accessed=half * units * 12 + rows * half * 8,
            transcendentals=rows * units,
        ),
        name="expert_units",
    )(dp_index, modulation, own, left, right, *fars, *weights)


def weigh_kernel(y_ref, ids_ref, dropped_ref, normed_ref, mod_ref, router_ref, weight_ref, rank_ref):
    rows, _ = normed_ref.shape
    hidden_in = (
        normed_ref[...].astype(jnp.float32) * (1.0 + mod_ref[0:1, :]) + mod_ref[1:2, :]
    ).astype(jnp.bfloat16)
    gates = jax.nn.sigmoid(
        lax.dot_general(
            router_ref[...], hidden_in, TRANSPOSED, preferred_element_type=jnp.float32
        )
    )
    which = lax.broadcasted_iota(jnp.int32, gates.shape, 0)
    weights = []
    for offset in OFFSETS:
        expert = lax.rem(y_ref[0] + offset + SIDE, SIDE)
        gate = jnp.sum(jnp.where(which == expert, gates, 0.0), axis=0, keepdims=True)
        kept = jnp.zeros((1, rows), jnp.float32)
        for k in range(2):
            chosen = jnp.where(ids_ref[k : k + 1, :] == expert, 1.0, 0.0)
            kept = kept + chosen * (1.0 - dropped_ref[k : k + 1, :].astype(jnp.float32))
        weights.append(gate * kept)
    weight_ref[...] = jnp.concatenate(weights + weights, axis=0)
    rank_ref[...] = ranks(y_ref, ids_ref)


def weigh(y_index, ids, dropped, normed, modulation, router):
    rows, width = normed.shape
    return pl.pallas_call(
        weigh_kernel,
        out_shape=[jax.ShapeDtypeStruct((8, rows), jnp.float32)] * 2,
        in_specs=[in_smem()] + [in_vmem()] * 5,
        out_specs=[in_vmem()] * 2,
        compiler_params=pltpu.CompilerParams(vmem_limit_bytes=VMEM_LIMIT),
        cost_estimate=pl.CostEstimate(
            flops=2 * 128 * rows * width, bytes_accessed=4 * rows * width, transcendentals=0
        ),
        name="weigh",
    )(y_index, ids, dropped, normed, modulation, router)


def combine_kernel(counts, weight_ref, rank_ref, total_ref, *refs):
    out_ref = refs[-1]
    rows, width = out_ref.shape
    picks, scales = [], []
    for k in range(len(counts)):
        slots = refs[sum(counts[:k])].shape[1]
        slot = lax.broadcasted_iota(jnp.int32, (slots, rows), 0).astype(jnp.float32)
        pick = jnp.where(slot == rank_ref[k : k + 1, :], 1.0, 0.0)
        scales.append(jnp.sum(pick * weight_ref[k : k + 1, :], axis=1, keepdims=True))
        picks.append(pick.astype(jnp.bfloat16))
    half = width // 2
    tile = half // 2
    for start in range(0, width, tile):
        span = slice(start, start + tile)
        side, column = start // half, slice(start % half, start % half + tile)
        total = total_ref[:, span].astype(jnp.float32)
        first = 0
        for pick, scale, count in zip(picks, scales, counts):
            back = sum(
                ref[side, :, column].astype(jnp.float32) for ref in refs[first : first + count]
            )
            first += count
            total = total + lax.dot_general(
                pick,
                (back * scale).astype(jnp.bfloat16),
                (((0,), (0,)), ((), ())),
                preferred_element_type=jnp.float32,
            )
        out_ref[:, span] = total.astype(out_ref.dtype)


def combine(weight, rank, tokens, backs):
    rows, width = tokens.shape
    counts = [len(group) for group in backs]
    return pl.pallas_call(
        functools.partial(combine_kernel, counts),
        out_shape=jax.ShapeDtypeStruct((rows, width), jnp.bfloat16),
        in_specs=[in_vmem()] * (3 + sum(counts)),
        out_specs=in_vmem(),
        compiler_params=pltpu.CompilerParams(vmem_limit_bytes=VMEM_LIMIT),
        cost_estimate=pl.CostEstimate(
            flops=2 * len(backs) * SLOTS * rows * width,
            bytes_accessed=10 * rows * width,
            transcendentals=0,
        ),
        name="add_terms",
    )(weight, rank, tokens, *sum(backs, []))


def on_device(
    tokens,
    text_states,
    text_lengths,
    mod_weight,
    router_weight,
    gate_weight,
    up_weight,
    down_weight,
    expert_ids,
    dropped,
):
    _, rows, width = tokens.shape
    tokens = tokens[0]
    ids = expert_ids[0].T
    owners = lax.axis_size("expert")
    y_index = (lax.axis_index("expert") // SIDE).astype(jnp.int32).reshape(1)
    dp_index = lax.axis_index("dp").astype(jnp.int32).reshape(1)

    def exchange(value, axis="expert"):
        return lax.all_to_all(value, axis, split_axis=0, concat_axis=0, tiled=True)

    normed, *bins = make_bins(y_index, ids, tokens)
    bins = dict(zip(OFFSETS, bins))

    positions = jnp.arange(text_states.shape[1], dtype=jnp.int32)
    valid = (positions[None, :] < text_lengths[:, None]).astype(jnp.bfloat16)
    pooled = jnp.einsum("it,itc->ic", valid, text_states, preferred_element_type=jnp.float32)
    pooled = (pooled / text_lengths.astype(jnp.float32)[:, None]).astype(jnp.bfloat16)
    partial_value = jnp.dot(pooled, mod_weight, preferred_element_type=jnp.float32)

    tie = lax.optimization_barrier
    left_of, right_of, across_x = along_x(-1), along_x(1), along_x(2)

    def both_ways(value):
        return shift(value, right_of), shift(value, left_of)

    def add_half(value, side, extra):
        halves = [value[0], value[1]]
        halves[side] = halves[side] + extra
        return jnp.stack(halves)

    def total_of(*parts):
        return sum(part.astype(jnp.float32) for part in parts).astype(jnp.bfloat16)

    def run(own, near, far):
        return run_expert(dp_index, modulation, own, *near, far, weights)

    middle = bins[0]
    from_up, from_down = shift(bins[1], along_y(1)), shift(bins[-1], along_y(-1))
    from_up, from_down, partial_value, *middle_near = tie(
        (from_up, from_down, partial_value, *both_ways(middle))
    )

    sides = pack(from_up, from_down)
    near = both_ways(sides)
    swap = [(0, 1), (1, 0)]
    owns = tie((gate_weight.T, up_weight.T, down_weight, from_up))[:3]
    swapped = [lax.ppermute(own, "dp", swap) for own in owns]
    columns = jnp.sum(exchange(partial_value, "seq"), axis=0, keepdims=True)
    columns, outer, *rest = tie((columns, bins[2], *near, *swapped))
    near, swapped = rest[:2], rest[2:]
    weights = [owns[0], swapped[0], owns[1], swapped[1], owns[2], swapped[2]]

    far = shift(near[0][0], right_of), shift(near[1][1], left_of)
    outer = shift(outer, along_y(2))
    modulation = exchange(jnp.broadcast_to(columns, (owners, columns.shape[1]))).reshape(2, width)
    modulation, outer, middle, *far = tie((modulation, outer, middle, *far))

    outer_near, outer_far = both_ways(outer), shift(outer, across_x)
    middle_far = shift(middle, across_x)
    out_sides = run(sides, near, far)
    middle_far, outer_far, *rest = tie((middle_far, outer_far, *outer_near, *out_sides))
    outer_near, out_sides = rest[:2], rest[2:]

    got = shift(out_sides[3][0], left_of), shift(out_sides[3][1], right_of)
    out_outer = run(outer, outer_near, (outer_far,))
    rest = tie((*got, *out_outer))
    got, out_outer = rest[:2], rest[2:]

    sums = (
        shift(add_half(out_sides[1], 0, got[0]), left_of),
        shift(add_half(out_sides[2], 1, got[1]), right_of),
    )
    got = shift(out_outer[3][0], left_of), shift(out_outer[3][1], right_of)
    out_middle = run(middle, middle_near, (middle_far,))
    rest = tie((*sums, *got, *out_middle))
    sums, got, out_middle = rest[:2], rest[2:4], rest[4:]

    outer_sums = (
        shift(add_half(out_outer[1], 0, got[0]), left_of),
        shift(add_half(out_outer[2], 1, got[1]), right_of),
    )
    back = total_of(out_sides[0], *sums)
    backs = {
        1: [shift(back[:, :MOST], along_y(-1))],
        -1: [shift(back[:, MOST:], along_y(1))],
    }
    middle_far = shift(out_middle[3], across_x)
    outer_back = total_of(out_outer[0], *outer_sums)
    to_left, to_right, outer_back = tie((out_middle[1], out_middle[2], outer_back))
    middle_sums = middle_far, shift(to_left, left_of), shift(to_right, right_of)
    weight, rank = weigh(y_index, ids, dropped[0].T, normed, modulation, router_weight.T)
    backs[2] = [shift(outer_back, along_y(2))]
    backs[0] = [out_middle[0], *middle_sums]
    total = combine(weight, rank, tokens, [backs[offset] for offset in OFFSETS])
    return total[None]


def solution(mesh):
    return jax.shard_map(
        on_device,
        mesh=mesh,
        in_specs=(
            P(("dp", "seq"), "expert", None),
            P("dp", None, "seq"),
            P("dp"),
            P("seq", "expert"),
            P(),
            P("dp", "expert"),
            P("dp", "expert"),
            P("expert", "dp"),
            P(("dp", "seq"), "expert", None),
            P(("dp", "seq"), "expert", None),
        ),
        out_specs=P(("dp", "seq"), "expert", None),
        check_vma=False,
    )
```

```python
import functools

import jax
import jax.numpy as jnp
from jax import lax
from jax.experimental import pallas as pl
from jax.experimental.pallas import tpu as pltpu
from jax.sharding import PartitionSpec as P

SIDE = 4
SLOTS = 72
MOST = 68
OFFSETS = (0, 1, -1, 2)
BAND = 256
VMEM_LIMIT = 20 * 1024 * 1024
TRANSPOSED = (((1,), (1,)), ((), ()))


def along_x(step):
    return [
        (y * SIDE + x, y * SIDE + (x + step) % SIDE) for y in range(SIDE) for x in range(SIDE)
    ]


def along_y(step):
    return [
        (y * SIDE + x, ((y + step) % SIDE) * SIDE + x) for y in range(SIDE) for x in range(SIDE)
    ]


def shift(value, perm):
    return lax.ppermute(value, "expert", perm)


def after(value, *others):
    return lax.optimization_barrier((value,) + others)[0]


def in_vmem():
    return pl.BlockSpec(memory_space=pltpu.VMEM)


def in_smem():
    return pl.BlockSpec(memory_space=pltpu.SMEM)


def ranks(y_ref, ids_ref):
    rows = ids_ref.shape[1]
    before = (
        lax.broadcasted_iota(jnp.int32, (rows, rows), 0)
        < lax.broadcasted_iota(jnp.int32, (rows, rows), 1)
    ).astype(jnp.bfloat16)
    place = lax.broadcasted_iota(jnp.int32, (8, rows), 0)
    expert = jnp.full((8, rows), -1, jnp.int32)
    for k, offset in enumerate(OFFSETS):
        expert = jnp.where(place == k, lax.rem(y_ref[0] + offset + SIDE, SIDE), expert)
    named = jnp.where((ids_ref[0:1, :] == expert) | (ids_ref[1:2, :] == expert), 1.0, 0.0)
    rank = jnp.dot(named.astype(jnp.bfloat16), before, preferred_element_type=jnp.float32)
    return jnp.where(named > 0.0, rank, -1.0)


def bin_kernel(y_ref, ids_ref, tokens_ref, normed_ref, *bin_refs):
    rows, width = tokens_ref.shape
    for start in range(0, rows, 16):
        block = tokens_ref[start : start + 16, :].astype(jnp.float32)
        centre = jnp.sum(block, axis=1, keepdims=True) * (1.0 / width)
        block = block - centre
        spread = jnp.sum(block * block, axis=1, keepdims=True) * (1.0 / width)
        normed_ref[start : start + 16, :] = (block * lax.rsqrt(spread + 1e-06)).astype(
            jnp.bfloat16
        )
    rank = ranks(y_ref, ids_ref)
    slot = lax.broadcasted_iota(jnp.int32, (SLOTS, rows), 0).astype(jnp.float32)
    normed = normed_ref[...]
    for k, bin_ref in enumerate(bin_refs):
        pick = jnp.where(slot == rank[k : k + 1, :], 1.0, 0.0).astype(jnp.bfloat16)
        for half in range(2):
            span = slice(half * (width // 2), (half + 1) * (width // 2))
            bin_ref[half] = jnp.dot(
                pick, normed[:, span], preferred_element_type=jnp.float32
            ).astype(jnp.bfloat16)


def make_bins(y_index, ids_rows, tokens):
    rows, width = tokens.shape
    return pl.pallas_call(
        bin_kernel,
        out_shape=[jax.ShapeDtypeStruct((rows, width), jnp.bfloat16)]
        + [jax.ShapeDtypeStruct((2, SLOTS, width // 2), jnp.bfloat16)] * len(OFFSETS),
        in_specs=[in_smem(), in_vmem(), in_vmem()],
        out_specs=[in_vmem()] * (1 + len(OFFSETS)),
        compiler_params=pltpu.CompilerParams(vmem_limit_bytes=VMEM_LIMIT),
        cost_estimate=pl.CostEstimate(
            flops=2 * 4 * SLOTS * rows * width, bytes_accessed=8 * rows * width, transcendentals=0
        ),
        name="normalise_and_bin",
    )(y_index, ids_rows, tokens)


def pack_kernel(first_ref, second_ref, out_ref):
    row = lax.broadcasted_iota(jnp.int32, (2 * MOST, SLOTS), 0)
    column = lax.broadcasted_iota(jnp.int32, (2 * MOST, SLOTS), 1)
    first = ((row == column) & (row < MOST)).astype(jnp.bfloat16)
    second = (row == column + MOST).astype(jnp.bfloat16)
    for side in range(2):
        out_ref[side] = (
            jnp.dot(first, first_ref[side], preferred_element_type=jnp.float32)
            + jnp.dot(second, second_ref[side], preferred_element_type=jnp.float32)
        ).astype(jnp.bfloat16)


def pack(first, second):
    _, slots, half = first.shape
    return pl.pallas_call(
        pack_kernel,
        out_shape=jax.ShapeDtypeStruct((2, 2 * MOST, half), jnp.bfloat16),
        in_specs=[in_vmem()] * 2,
        out_specs=in_vmem(),
        compiler_params=pltpu.CompilerParams(vmem_limit_bytes=VMEM_LIMIT),
        cost_estimate=pl.CostEstimate(
            flops=16 * MOST * slots * half, bytes_accessed=16 * MOST * half, transcendentals=0
        ),
        name="pack",
    )(first, second)


def expert_kernel(
    dp_ref,
    mod_ref,
    own_ref,
    left_ref,
    right_ref,
    *refs,
):
    *far_refs, gate_own, gate_far, up_own, up_far, down_own, down_far = refs[:-6]
    out_own, out_left, out_right, out_far, hidden_in, hidden = refs[-6:]
    _, size, half = own_ref.shape
    units = gate_own.shape[0]
    banks = (dp_ref[0], 1 - dp_ref[0])
    for side in range(2):
        far_ref = far_refs[side] if len(far_refs) == 2 else far_refs[0].at[side]

        def prepare(step, carry, side=side, far_ref=far_ref):
            start = pl.multiple_of(step * BAND, BAND)
            span = pl.ds(start, BAND)
            column = pl.ds(pl.multiple_of(side * half + start, BAND), BAND)
            blocks = [ref[side, :, span] for ref in (own_ref, left_ref, right_ref)]
            values = jnp.concatenate(
                [block.astype(jnp.float32) for block in blocks + [far_ref[:, span]]], axis=0
            )
            hidden_in[banks[side], :, span] = (
                values * (1.0 + mod_ref[0:1, column]) + mod_ref[1:2, column]
            ).astype(jnp.bfloat16)
            return carry

        lax.fori_loop(0, half // BAND, prepare, 0)

    def band(start, count):
        span = pl.ds(start, count)
        both = 0.0
        for bank, (gate, up) in enumerate(((gate_own, up_own), (gate_far, up_far))):
            both = both + lax.dot_general(
                hidden_in[bank],
                jnp.concatenate([gate[span, :], up[span, :]], axis=0),
                TRANSPOSED,
                preferred_element_type=jnp.float32,
            )
        hidden[:, span] = (jax.nn.silu(both[:, :count]) * both[:, count:]).astype(jnp.bfloat16)

    def full_band(step, carry):
        band(pl.multiple_of(step * BAND, BAND), BAND)
        return carry

    lax.fori_loop(0, units // BAND, full_band, 0)
    if units % BAND:
        band(units - units % BAND, units % BAND)
    tile = half // 2
    outs = (out_own, out_left, out_right, out_far)
    for bank, down in enumerate((down_own, down_far)):

        def project(step, carry, bank=bank, down=down):
            span = pl.ds(pl.multiple_of(step * tile, tile), tile)
            out = jnp.dot(hidden[...], down[:, span], preferred_element_type=jnp.float32)
            for k, out_ref in enumerate(outs):
                out_ref[banks[bank], :, span] = out[k * size : (k + 1) * size].astype(
                    jnp.bfloat16
                )
            return carry

        lax.fori_loop(0, half // tile, project, 0)


def run_expert(dp_index, modulation, own, left, right, fars, weights):
    _, size, half = own.shape
    units = weights[0].shape[0]
    rows = SIDE * size
    return pl.pallas_call(
        expert_kernel,
        out_shape=[jax.ShapeDtypeStruct(own.shape, jnp.bfloat16)] * 4,
        in_specs=[in_smem()] + [in_vmem()] * (4 + len(fars) + len(weights)),
        out_specs=[in_vmem()] * 4,
        scratch_shapes=[
            pltpu.VMEM((2, rows, half), jnp.bfloat16),
            pltpu.VMEM((rows, units), jnp.bfloat16),
        ],
        compiler_params=pltpu.CompilerParams(vmem_limit_bytes=VMEM_LIMIT),
        cost_estimate=pl.CostEstimate(
            flops=rows * half * units * 24,
            bytes_accessed=half * units * 12 + rows * half * 8,
            transcendentals=rows * units,
        ),
        name="expert_units",
    )(dp_index, modulation, own, left, right, *fars, *weights)


def weigh_kernel(y_ref, ids_ref, dropped_ref, normed_ref, mod_ref, router_ref, weight_ref, rank_ref):
    rows, _ = normed_ref.shape
    hidden_in = (
        normed_ref[...].astype(jnp.float32) * (1.0 + mod_ref[0:1, :]) + mod_ref[1:2, :]
    ).astype(jnp.bfloat16)
    gates = jax.nn.sigmoid(
        lax.dot_general(
            router_ref[...], hidden_in, TRANSPOSED, preferred_element_type=jnp.float32
        )
    )
    which = lax.broadcasted_iota(jnp.int32, gates.shape, 0)
    weights = []
    for offset in OFFSETS:
        expert = lax.rem(y_ref[0] + offset + SIDE, SIDE)
        gate = jnp.sum(jnp.where(which == expert, gates, 0.0), axis=0, keepdims=True)
        kept = jnp.zeros((1, rows), jnp.float32)
        for k in range(2):
            chosen = jnp.where(ids_ref[k : k + 1, :] == expert, 1.0, 0.0)
            kept = kept + chosen * (1.0 - dropped_ref[k : k + 1, :].astype(jnp.float32))
        weights.append(gate * kept)
    weight_ref[...] = jnp.concatenate(weights + weights, axis=0)
    rank_ref[...] = ranks(y_ref, ids_ref)


def weigh(y_index, ids, dropped, normed, modulation, router):
    rows, width = normed.shape
    return pl.pallas_call(
        weigh_kernel,
        out_shape=[jax.ShapeDtypeStruct((8, rows), jnp.float32)] * 2,
        in_specs=[in_smem()] + [in_vmem()] * 5,
        out_specs=[in_vmem()] * 2,
        compiler_params=pltpu.CompilerParams(vmem_limit_bytes=VMEM_LIMIT),
        cost_estimate=pl.CostEstimate(
            flops=2 * 128 * rows * width, bytes_accessed=4 * rows * width, transcendentals=0
        ),
        name="weigh",
    )(y_index, ids, dropped, normed, modulation, router)


def combine_kernel(counts, weight_ref, rank_ref, total_ref, *refs):
    out_ref = refs[-1]
    rows, width = out_ref.shape
    picks, scales = [], []
    for k in range(len(counts)):
        slots = refs[sum(counts[:k])].shape[1]
        slot = lax.broadcasted_iota(jnp.int32, (slots, rows), 0).astype(jnp.float32)
        pick = jnp.where(slot == rank_ref[k : k + 1, :], 1.0, 0.0)
        scales.append(jnp.sum(pick * weight_ref[k : k + 1, :], axis=1, keepdims=True))
        picks.append(pick.astype(jnp.bfloat16))
    half = width // 2
    tile = half // 2
    for start in range(0, width, tile):
        span = slice(start, start + tile)
        side, column = start // half, slice(start % half, start % half + tile)
        total = total_ref[:, span].astype(jnp.float32)
        first = 0
        for pick, scale, count in zip(picks, scales, counts):
            back = sum(
                ref[side, :, column].astype(jnp.float32) for ref in refs[first : first + count]
            )
            first += count
            total = total + lax.dot_general(
                pick,
                (back * scale).astype(jnp.bfloat16),
                (((0,), (0,)), ((), ())),
                preferred_element_type=jnp.float32,
            )
        out_ref[:, span] = total.astype(out_ref.dtype)


def combine(weight, rank, tokens, backs):
    rows, width = tokens.shape
    counts = [len(group) for group in backs]
    return pl.pallas_call(
        functools.partial(combine_kernel, counts),
        out_shape=jax.ShapeDtypeStruct((rows, width), jnp.bfloat16),
        in_specs=[in_vmem()] * (3 + sum(counts)),
        out_specs=in_vmem(),
        compiler_params=pltpu.CompilerParams(vmem_limit_bytes=VMEM_LIMIT),
        cost_estimate=pl.CostEstimate(
            flops=2 * len(backs) * SLOTS * rows * width,
            bytes_accessed=10 * rows * width,
            transcendentals=0,
        ),
        name="add_terms",
    )(weight, rank, tokens, *sum(backs, []))


def on_device(
    tokens,
    text_states,
    text_lengths,
    mod_weight,
    router_weight,
    gate_weight,
    up_weight,
    down_weight,
    expert_ids,
    dropped,
):
    _, rows, width = tokens.shape
    tokens = tokens[0]
    ids = expert_ids[0].T
    owners = lax.axis_size("expert")
    y_index = (lax.axis_index("expert") // SIDE).astype(jnp.int32).reshape(1)
    dp_index = lax.axis_index("dp").astype(jnp.int32).reshape(1)

    def exchange(value, axis="expert"):
        return lax.all_to_all(value, axis, split_axis=0, concat_axis=0, tiled=True)

    normed, *bins = make_bins(y_index, ids, tokens)
    bins = dict(zip(OFFSETS, bins))

    positions = jnp.arange(text_states.shape[1], dtype=jnp.int32)
    valid = (positions[None, :] < text_lengths[:, None]).astype(jnp.bfloat16)
    pooled = jnp.einsum("it,itc->ic", valid, text_states, preferred_element_type=jnp.float32)
    pooled = (pooled / text_lengths.astype(jnp.float32)[:, None]).astype(jnp.bfloat16)
    partial_value = jnp.dot(pooled, mod_weight, preferred_element_type=jnp.float32)

    tie = lax.optimization_barrier
    left_of, right_of, across_x = along_x(-1), along_x(1), along_x(2)

    def both_ways(value):
        return shift(value, right_of), shift(value, left_of)

    def add_half(value, side, extra):
        halves = [value[0], value[1]]
        halves[side] = halves[side] + extra
        return jnp.stack(halves)

    def total_of(*parts):
        return sum(part.astype(jnp.float32) for part in parts).astype(jnp.bfloat16)

    def run(own, near, far):
        return run_expert(dp_index, modulation, own, *near, far, weights)

    middle = bins[0]
    from_up, from_down = shift(bins[1], along_y(1)), shift(bins[-1], along_y(-1))
    from_up, from_down, partial_value, *middle_near = tie(
        (from_up, from_down, partial_value, *both_ways(middle))
    )

    sides = pack(from_up, from_down)
    near = both_ways(sides)
    swap = [(0, 1), (1, 0)]
    owns = tie((gate_weight.T, up_weight.T, down_weight, from_up))[:3]
    swapped = [lax.ppermute(own, "dp", swap) for own in owns]
    columns = jnp.sum(exchange(partial_value, "seq"), axis=0, keepdims=True)
    columns, outer, *rest = tie((columns, bins[2], *near, *swapped))
    near, swapped = rest[:2], rest[2:]
    weights = [owns[0], swapped[0], owns[1], swapped[1], owns[2], swapped[2]]

    far = shift(near[0][0], right_of), shift(near[1][1], left_of)
    outer = shift(outer, along_y(2))
    modulation = exchange(jnp.broadcast_to(columns, (owners, columns.shape[1]))).reshape(2, width)
    modulation, outer, middle, *far = tie((modulation, outer, middle, *far))

    outer_near, outer_far = both_ways(outer), shift(outer, across_x)
    middle_far = shift(middle, across_x)
    out_sides = run(sides, near, far)
    middle_far, outer_far, *rest = tie((middle_far, outer_far, *outer_near, *out_sides))
    outer_near, out_sides = rest[:2], rest[2:]

    got = shift(out_sides[3][0], left_of), shift(out_sides[3][1], right_of)
    out_outer = run(outer, outer_near, (outer_far,))
    rest = tie((*got, *out_outer))
    got, out_outer = rest[:2], rest[2:]

    sums = (
        shift(add_half(out_sides[1], 0, got[0]), left_of),
        shift(add_half(out_sides[2], 1, got[1]), right_of),
    )
    got = shift(out_outer[3][0], left_of), shift(out_outer[3][1], right_of)
    out_middle = run(middle, middle_near, (middle_far,))
    rest = tie((*sums, *got, *out_middle))
    sums, got, out_middle = rest[:2], rest[2:4], rest[4:]

    outer_sums = (
        shift(add_half(out_outer[1], 0, got[0]), left_of),
        shift(add_half(out_outer[2], 1, got[1]), right_of),
    )
    back = total_of(out_sides[0], *sums)
    backs = {
        1: [shift(back[:, :MOST], along_y(-1))],
        -1: [shift(back[:, MOST:], along_y(1))],
    }
    middle_far = shift(out_middle[3], across_x)
    outer_back = total_of(out_outer[0], *outer_sums)
    to_left, to_right, outer_back, *sides_back = tie(
        (out_middle[1], out_middle[2], outer_back, backs[1][0], backs[-1][0])
    )
    backs = {1: sides_back[:1], -1: sides_back[1:]}
    middle_sums = middle_far, shift(to_left, left_of), shift(to_right, right_of)
    weight, rank = weigh(y_index, ids, dropped[0].T, normed, modulation, router_weight.T)
    backs[2] = [shift(outer_back, along_y(2))]
    backs[0] = [out_middle[0], *middle_sums]
    total = combine(weight, rank, tokens, [backs[offset] for offset in OFFSETS])
    return total[None]


def solution(mesh):
    return jax.shard_map(
        on_device,
        mesh=mesh,
        in_specs=(
            P(("dp", "seq"), "expert", None),
            P("dp", None, "seq"),
            P("dp"),
            P("seq", "expert"),
            P(),
            P("dp", "expert"),
            P("dp", "expert"),
            P("expert", "dp"),
            P(("dp", "seq"), "expert", None),
            P(("dp", "seq"), "expert", None),
        ),
        out_specs=P(("dp", "seq"), "expert", None),
        check_vma=False,
    )
```

```python
import functools

import jax
import jax.numpy as jnp
from jax import lax
from jax.experimental import pallas as pl
from jax.experimental.pallas import tpu as pltpu
from jax.sharding import PartitionSpec as P

SIDE = 4
SLOTS = 72
MOST = 68
OFFSETS = (0, 1, -1, 2)
BAND = 256
VMEM_LIMIT = 20 * 1024 * 1024
TRANSPOSED = (((1,), (1,)), ((), ()))


def along_x(step):
    return [
        (y * SIDE + x, y * SIDE + (x + step) % SIDE) for y in range(SIDE) for x in range(SIDE)
    ]


def along_y(step):
    return [
        (y * SIDE + x, ((y + step) % SIDE) * SIDE + x) for y in range(SIDE) for x in range(SIDE)
    ]


def shift(value, perm):
    return lax.ppermute(value, "expert", perm)


def after(value, *others):
    return lax.optimization_barrier((value,) + others)[0]


def in_vmem():
    return pl.BlockSpec(memory_space=pltpu.VMEM)


def in_smem():
    return pl.BlockSpec(memory_space=pltpu.SMEM)


def ranks(y_ref, ids_ref):
    rows = ids_ref.shape[1]
    before = (
        lax.broadcasted_iota(jnp.int32, (rows, rows), 0)
        < lax.broadcasted_iota(jnp.int32, (rows, rows), 1)
    ).astype(jnp.bfloat16)
    place = lax.broadcasted_iota(jnp.int32, (8, rows), 0)
    expert = jnp.full((8, rows), -1, jnp.int32)
    for k, offset in enumerate(OFFSETS):
        expert = jnp.where(place == k, lax.rem(y_ref[0] + offset + SIDE, SIDE), expert)
    named = jnp.where((ids_ref[0:1, :] == expert) | (ids_ref[1:2, :] == expert), 1.0, 0.0)
    rank = jnp.dot(named.astype(jnp.bfloat16), before, preferred_element_type=jnp.float32)
    return jnp.where(named > 0.0, rank, -1.0)


def bin_kernel(y_ref, ids_ref, tokens_ref, normed_ref, *bin_refs):
    rows, width = tokens_ref.shape
    for start in range(0, rows, 16):
        block = tokens_ref[start : start + 16, :].astype(jnp.float32)
        centre = jnp.sum(block, axis=1, keepdims=True) * (1.0 / width)
        block = block - centre
        spread = jnp.sum(block * block, axis=1, keepdims=True) * (1.0 / width)
        normed_ref[start : start + 16, :] = (block * lax.rsqrt(spread + 1e-06)).astype(
            jnp.bfloat16
        )
    rank = ranks(y_ref, ids_ref)
    slot = lax.broadcasted_iota(jnp.int32, (SLOTS, rows), 0).astype(jnp.float32)
    normed = normed_ref[...]
    for k, bin_ref in enumerate(bin_refs):
        pick = jnp.where(slot == rank[k : k + 1, :], 1.0, 0.0).astype(jnp.bfloat16)
        for half in range(2):
            span = slice(half * (width // 2), (half + 1) * (width // 2))
            bin_ref[half] = jnp.dot(
                pick, normed[:, span], preferred_element_type=jnp.float32
            ).astype(jnp.bfloat16)


def make_bins(y_index, ids_rows, tokens):
    rows, width = tokens.shape
    return pl.pallas_call(
        bin_kernel,
        out_shape=[jax.ShapeDtypeStruct((rows, width), jnp.bfloat16)]
        + [jax.ShapeDtypeStruct((2, SLOTS, width // 2), jnp.bfloat16)] * len(OFFSETS),
        in_specs=[in_smem(), in_vmem(), in_vmem()],
        out_specs=[in_vmem()] * (1 + len(OFFSETS)),
        compiler_params=pltpu.CompilerParams(vmem_limit_bytes=VMEM_LIMIT),
        cost_estimate=pl.CostEstimate(
            flops=2 * 4 * SLOTS * rows * width, bytes_accessed=8 * rows * width, transcendentals=0
        ),
        name="normalise_and_bin",
    )(y_index, ids_rows, tokens)


def pack_kernel(first_ref, second_ref, out_ref):
    row = lax.broadcasted_iota(jnp.int32, (2 * MOST, SLOTS), 0)
    column = lax.broadcasted_iota(jnp.int32, (2 * MOST, SLOTS), 1)
    first = ((row == column) & (row < MOST)).astype(jnp.bfloat16)
    second = (row == column + MOST).astype(jnp.bfloat16)
    for side in range(2):
        out_ref[side] = (
            jnp.dot(first, first_ref[side], preferred_element_type=jnp.float32)
            + jnp.dot(second, second_ref[side], preferred_element_type=jnp.float32)
        ).astype(jnp.bfloat16)


def pack(first, second):
    _, slots, half = first.shape
    return pl.pallas_call(
        pack_kernel,
        out_shape=jax.ShapeDtypeStruct((2, 2 * MOST, half), jnp.bfloat16),
        in_specs=[in_vmem()] * 2,
        out_specs=in_vmem(),
        compiler_params=pltpu.CompilerParams(vmem_limit_bytes=VMEM_LIMIT),
        cost_estimate=pl.CostEstimate(
            flops=16 * MOST * slots * half, bytes_accessed=16 * MOST * half, transcendentals=0
        ),
        name="pack",
    )(first, second)


def expert_kernel(
    dp_ref,
    mod_ref,
    own_ref,
    left_ref,
    right_ref,
    *refs,
):
    *far_refs, gate_own, gate_far, up_own, up_far, down_own, down_far = refs[:-6]
    out_own, out_left, out_right, out_far, hidden_in, hidden = refs[-6:]
    _, size, half = own_ref.shape
    units = gate_own.shape[0]
    banks = (dp_ref[0], 1 - dp_ref[0])
    for side in range(2):
        far_ref = far_refs[side] if len(far_refs) == 2 else far_refs[0].at[side]

        def prepare(step, carry, side=side, far_ref=far_ref):
            start = pl.multiple_of(step * BAND, BAND)
            span = pl.ds(start, BAND)
            column = pl.ds(pl.multiple_of(side * half + start, BAND), BAND)
            blocks = [ref[side, :, span] for ref in (own_ref, left_ref, right_ref)]
            values = jnp.concatenate(
                [block.astype(jnp.float32) for block in blocks + [far_ref[:, span]]], axis=0
            )
            hidden_in[banks[side], :, span] = (
                values * (1.0 + mod_ref[0:1, column]) + mod_ref[1:2, column]
            ).astype(jnp.bfloat16)
            return carry

        lax.fori_loop(0, half // BAND, prepare, 0)

    def band(start, count):
        span = pl.ds(start, count)
        both = 0.0
        for bank, (gate, up) in enumerate(((gate_own, up_own), (gate_far, up_far))):
            both = both + lax.dot_general(
                hidden_in[bank],
                jnp.concatenate([gate[span, :], up[span, :]], axis=0),
                TRANSPOSED,
                preferred_element_type=jnp.float32,
            )
        hidden[:, span] = (jax.nn.silu(both[:, :count]) * both[:, count:]).astype(jnp.bfloat16)

    def full_band(step, carry):
        band(pl.multiple_of(step * BAND, BAND), BAND)
        return carry

    lax.fori_loop(0, units // BAND, full_band, 0)
    if units % BAND:
        band(units - units % BAND, units % BAND)
    tile = half // 2
    outs = (out_own, out_left, out_right, out_far)
    for bank, down in enumerate((down_own, down_far)):

        def project(step, carry, bank=bank, down=down):
            span = pl.ds(pl.multiple_of(step * tile, tile), tile)
            out = jnp.dot(hidden[...], down[:, span], preferred_element_type=jnp.float32)
            for k, out_ref in enumerate(outs):
                out_ref[banks[bank], :, span] = out[k * size : (k + 1) * size].astype(
                    jnp.bfloat16
                )
            return carry

        lax.fori_loop(0, half // tile, project, 0)


def run_expert(dp_index, modulation, own, left, right, fars, weights):
    _, size, half = own.shape
    units = weights[0].shape[0]
    rows = SIDE * size
    return pl.pallas_call(
        expert_kernel,
        out_shape=[jax.ShapeDtypeStruct(own.shape, jnp.bfloat16)] * 4,
        in_specs=[in_smem()] + [in_vmem()] * (4 + len(fars) + len(weights)),
        out_specs=[in_vmem()] * 4,
        scratch_shapes=[
            pltpu.VMEM((2, rows, half), jnp.bfloat16),
            pltpu.VMEM((rows, units), jnp.bfloat16),
        ],
        compiler_params=pltpu.CompilerParams(vmem_limit_bytes=VMEM_LIMIT),
        cost_estimate=pl.CostEstimate(
            flops=rows * half * units * 24,
            bytes_accessed=half * units * 12 + rows * half * 8,
            transcendentals=rows * units,
        ),
        name="expert_units",
    )(dp_index, modulation, own, left, right, *fars, *weights)


def weigh_kernel(y_ref, ids_ref, dropped_ref, normed_ref, mod_ref, router_ref, weight_ref, rank_ref):
    rows, _ = normed_ref.shape
    hidden_in = (
        normed_ref[...].astype(jnp.float32) * (1.0 + mod_ref[0:1, :]) + mod_ref[1:2, :]
    ).astype(jnp.bfloat16)
    gates = jax.nn.sigmoid(
        lax.dot_general(
            router_ref[...], hidden_in, TRANSPOSED, preferred_element_type=jnp.float32
        )
    )
    which = lax.broadcasted_iota(jnp.int32, gates.shape, 0)
    weights = []
    for offset in OFFSETS:
        expert = lax.rem(y_ref[0] + offset + SIDE, SIDE)
        gate = jnp.sum(jnp.where(which == expert, gates, 0.0), axis=0, keepdims=True)
        kept = jnp.zeros((1, rows), jnp.float32)
        for k in range(2):
            chosen = jnp.where(ids_ref[k : k + 1, :] == expert, 1.0, 0.0)
            kept = kept + chosen * (1.0 - dropped_ref[k : k + 1, :].astype(jnp.float32))
        weights.append(gate * kept)
    weight_ref[...] = jnp.concatenate(weights + weights, axis=0)
    rank_ref[...] = ranks(y_ref, ids_ref)


def weigh(y_index, ids, dropped, normed, modulation, router):
    rows, width = normed.shape
    return pl.pallas_call(
        weigh_kernel,
        out_shape=[jax.ShapeDtypeStruct((8, rows), jnp.float32)] * 2,
        in_specs=[in_smem()] + [in_vmem()] * 5,
        out_specs=[in_vmem()] * 2,
        compiler_params=pltpu.CompilerParams(vmem_limit_bytes=VMEM_LIMIT),
        cost_estimate=pl.CostEstimate(
            flops=2 * 128 * rows * width, bytes_accessed=4 * rows * width, transcendentals=0
        ),
        name="weigh",
    )(y_index, ids, dropped, normed, modulation, router)


def combine_kernel(counts, weight_ref, rank_ref, total_ref, *refs):
    out_ref = refs[-1]
    rows, width = out_ref.shape
    picks, scales = [], []
    for k in range(len(counts)):
        slots = refs[sum(counts[:k])].shape[1]
        slot = lax.broadcasted_iota(jnp.int32, (slots, rows), 0).astype(jnp.float32)
        pick = jnp.where(slot == rank_ref[k : k + 1, :], 1.0, 0.0)
        scales.append(jnp.sum(pick * weight_ref[k : k + 1, :], axis=1, keepdims=True))
        picks.append(pick.astype(jnp.bfloat16))
    half = width // 2
    tile = half // 2
    for start in range(0, width, tile):
        span = slice(start, start + tile)
        side, column = start // half, slice(start % half, start % half + tile)
        total = total_ref[:, span].astype(jnp.float32)
        first = 0
        for pick, scale, count in zip(picks, scales, counts):
            back = sum(
                ref[side, :, column].astype(jnp.float32) for ref in refs[first : first + count]
            )
            first += count
            total = total + lax.dot_general(
                pick,
                (back * scale).astype(jnp.bfloat16),
                (((0,), (0,)), ((), ())),
                preferred_element_type=jnp.float32,
            )
        out_ref[:, span] = total.astype(out_ref.dtype)


def combine(weight, rank, tokens, backs):
    rows, width = tokens.shape
    counts = [len(group) for group in backs]
    return pl.pallas_call(
        functools.partial(combine_kernel, counts),
        out_shape=jax.ShapeDtypeStruct((rows, width), jnp.bfloat16),
        in_specs=[in_vmem()] * (3 + sum(counts)),
        out_specs=in_vmem(),
        compiler_params=pltpu.CompilerParams(vmem_limit_bytes=VMEM_LIMIT),
        cost_estimate=pl.CostEstimate(
            flops=2 * len(backs) * SLOTS * rows * width,
            bytes_accessed=10 * rows * width,
            transcendentals=0,
        ),
        name="add_terms",
    )(weight, rank, tokens, *sum(backs, []))


def on_device(
    tokens,
    text_states,
    text_lengths,
    mod_weight,
    router_weight,
    gate_weight,
    up_weight,
    down_weight,
    expert_ids,
    dropped,
):
    _, rows, width = tokens.shape
    tokens = tokens[0]
    ids = expert_ids[0].T
    owners = lax.axis_size("expert")
    y_index = (lax.axis_index("expert") // SIDE).astype(jnp.int32).reshape(1)
    dp_index = lax.axis_index("dp").astype(jnp.int32).reshape(1)

    def exchange(value, axis="expert"):
        return lax.all_to_all(value, axis, split_axis=0, concat_axis=0, tiled=True)

    normed, *bins = make_bins(y_index, ids, tokens)
    bins = dict(zip(OFFSETS, bins))

    positions = jnp.arange(text_states.shape[1], dtype=jnp.int32)
    valid = (positions[None, :] < text_lengths[:, None]).astype(jnp.bfloat16)
    pooled = jnp.einsum("it,itc->ic", valid, text_states, preferred_element_type=jnp.float32)
    pooled = (pooled / text_lengths.astype(jnp.float32)[:, None]).astype(jnp.bfloat16)
    partial_value = jnp.dot(pooled, mod_weight, preferred_element_type=jnp.float32)

    tie = lax.optimization_barrier
    left_of, right_of, across_x = along_x(-1), along_x(1), along_x(2)

    def both_ways(value):
        return shift(value, right_of), shift(value, left_of)

    def add_half(value, side, extra):
        halves = [value[0], value[1]]
        halves[side] = halves[side] + extra
        return jnp.stack(halves)

    def total_of(*parts):
        return sum(part.astype(jnp.float32) for part in parts).astype(jnp.bfloat16)

    def run(own, near, far):
        return run_expert(dp_index, modulation, own, *near, far, weights)

    middle = bins[0]
    from_up, from_down = shift(bins[1], along_y(1)), shift(bins[-1], along_y(-1))
    from_up, from_down, partial_value, *middle_near = tie(
        (from_up, from_down, partial_value, *both_ways(middle))
    )

    sides = pack(from_up, from_down)
    near = both_ways(sides)
    swap = [(0, 1), (1, 0)]
    owns = tie((gate_weight.T, up_weight.T, down_weight, from_up))[:3]
    swapped = [lax.ppermute(own, "dp", swap) for own in owns]
    columns = jnp.sum(exchange(partial_value, "seq"), axis=0, keepdims=True)
    columns = jnp.broadcast_to(columns, (owners, columns.shape[1]))
    columns, outer, *rest = tie((columns, bins[2], *near, *swapped))
    near, swapped = rest[:2], rest[2:]
    weights = [owns[0], swapped[0], owns[1], swapped[1], owns[2], swapped[2]]

    far = shift(near[0][0], right_of), shift(near[1][1], left_of)
    outer = shift(outer, along_y(2))
    modulation = exchange(columns)
    modulation, outer, middle, *far = tie((modulation, outer, middle, *far))
    modulation = modulation.reshape(2, width)

    outer_near, outer_far = both_ways(outer), shift(outer, across_x)
    middle_far = shift(middle, across_x)
    out_sides = run(sides, near, far)
    middle_far, outer_far, *rest = tie((middle_far, outer_far, *outer_near, *out_sides))
    outer_near, out_sides = rest[:2], rest[2:]

    got = shift(out_sides[3][0], left_of), shift(out_sides[3][1], right_of)
    out_outer = run(outer, outer_near, (outer_far,))
    rest = tie((*got, *out_outer))
    got, out_outer = rest[:2], rest[2:]

    sums = (
        shift(add_half(out_sides[1], 0, got[0]), left_of),
        shift(add_half(out_sides[2], 1, got[1]), right_of),
    )
    got = shift(out_outer[3][0], left_of), shift(out_outer[3][1], right_of)
    out_middle = run(middle, middle_near, (middle_far,))
    rest = tie((*sums, *got, *out_middle))
    sums, got, out_middle = rest[:2], rest[2:4], rest[4:]

    outer_sums = (
        shift(add_half(out_outer[1], 0, got[0]), left_of),
        shift(add_half(out_outer[2], 1, got[1]), right_of),
    )
    back = total_of(out_sides[0], *sums)
    backs = {
        1: [shift(back[:, :MOST], along_y(-1))],
        -1: [shift(back[:, MOST:], along_y(1))],
    }
    middle_far = shift(out_middle[3], across_x)
    outer_back = total_of(out_outer[0], *outer_sums)
    to_left, to_right, outer_back, *sides_back = tie(
        (out_middle[1], out_middle[2], outer_back, backs[1][0], backs[-1][0])
    )
    backs = {1: sides_back[:1], -1: sides_back[1:]}
    middle_sums = middle_far, shift(to_left, left_of), shift(to_right, right_of)
    weight, rank = weigh(y_index, ids, dropped[0].T, normed, modulation, router_weight.T)
    backs[2] = [shift(outer_back, along_y(2))]
    backs[0] = [out_middle[0], *middle_sums]
    total = combine(weight, rank, tokens, [backs[offset] for offset in OFFSETS])
    return total[None]


def solution(mesh):
    return jax.shard_map(
        on_device,
        mesh=mesh,
        in_specs=(
            P(("dp", "seq"), "expert", None),
            P("dp", None, "seq"),
            P("dp"),
            P("seq", "expert"),
            P(),
            P("dp", "expert"),
            P("dp", "expert"),
            P("expert", "dp"),
            P(("dp", "seq"), "expert", None),
            P(("dp", "seq"), "expert", None),
        ),
        out_specs=P(("dp", "seq"), "expert", None),
        check_vma=False,
    )
```
